512 devices in a mesh: fibre: 64 (over x, z, core), tm: 8 (over y).
Axes of the slice: x: 4, y: 8, z: 8, core: 2. Of those that a mesh axis runs over, the one named last changes fastest.
Arguments:
- recordings: float32 [8, 64, 6000, 128], P('tm', 'fibre'), may hold values from -100 to 100
- pair_blocks: int32 [64, 4, 2], P('fibre'), may hold values from 0 to 63, as said below
- pair_count: int32 [64], P('fibre'), may hold values from 1 to 4, as said below
Outputs:
- stacks: float32 [64, 8, 401, 128], P('fibre', 'tm')
The draws below stay inside these ranges and needn't reach their ends.
Inputs may be any that keep to these rules, and one draw needn't show every extreme that they name: `pair_blocks`: every entry of owner o's list, live or not, lies in o .. min(o + 4, 63). `pair_count`: some owner has 4 live pairs in every draw.
All inputs are finite; a program needn't handle non-finite values.
Results may differ from the reference program's by a relative error of at most 0.0037.
Values may be sent and summed in bfloat16 or wider, within the bound.
No kernel may reach another device: no remote copies, remote signals or barrier semaphores. Data moves between devices by JAX's collectives and lax.ppermute only.
A program may use at most 64 MiB of HBM per device.

```python
import math
import jax
import jax.numpy as jnp
from jax import lax

CH = 128
TS = 6000
F0 = 60
NF = 1152
MAXLAG = 200
LAGS = 401
VS = 2
REACH = 4
MAXP = 4
WINDOWS = 8
NB = 64


def pair_tables(key):
    key_heavy, key_pick, key_first, key_second = jax.random.split(key, 4)
    owners = jnp.arange(NB, dtype=jnp.int32)
    heavy = jax.random.randint(key_heavy, (NB,), 0, 4) == 0
    chosen = jax.random.randint(key_pick, (), 0, NB)
    heavy = jnp.logical_or(heavy, owners == chosen)
    counts = jnp.where(heavy, MAXP, 1).astype(jnp.int32)
    avail = (jnp.minimum(REACH, NB - 1 - owners) + 1)[:, None]
    first_block = owners[:, None] + jax.random.randint(key_first, (NB, MAXP), 0, avail)
    second_block = owners[:, None] + jax.random.randint(key_second, (NB, MAXP), 0, avail)
    live_slots = jnp.arange(MAXP, dtype=jnp.int32)[None, :] < counts[:, None]
    first_block = jnp.where(live_slots, first_block, owners[:, None])
    second_block = jnp.where(live_slots, second_block, owners[:, None])
    return (jnp.stack([first_block, second_block], axis=-1).astype(jnp.int32), counts)


def draw_pair_blocks(key, part):
    tables = pair_tables(key)
    return tables[0]


def draw_pair_count(key, part):
    tables = pair_tables(key)
    return tables[1]


def draw_recordings(key, part):
    key = jax.random.fold_in(key, 11)
    key_noise, key_scale = jax.random.split(key, 2)
    scales = jnp.exp(jax.random.uniform(key_scale, (1, NB, 1, CH), jnp.float32, 0.0, math.log(10.0)))
    noise = jnp.clip(jax.random.normal(key_noise, (WINDOWS, NB, TS, CH), jnp.float32), -6.0, 6.0)
    return noise * scales


def setup_inputs(seed: int = 0) -> dict:
    key_of = jax.random.split(jax.random.key(seed), 4)
    recordings = draw_recordings(jax.random.fold_in(key_of[3], 71), 0)
    pair_blocks = draw_pair_blocks(jax.random.fold_in(key_of[3], 71), 0)
    pair_count = draw_pair_count(jax.random.fold_in(key_of[3], 71), 0)
    return dict(recordings=recordings, pair_blocks=pair_blocks, pair_count=pair_count)


EPSILON = 1e-06

def whiten(real_part, imag_part):
    power = lax.optimization_barrier(jnp.mean(real_part * real_part + imag_part * imag_part, axis=-2, keepdims=True))
    factor = lax.rsqrt(power + EPSILON)
    return jnp.concatenate([real_part * factor, imag_part * factor], axis=-2).astype(jnp.bfloat16)

def lag_table():
    lag_values = jnp.arange(LAGS, dtype=jnp.int32) - MAXLAG
    bin_values = jnp.arange(NF, dtype=jnp.int32) + F0
    phase = jnp.mod(lag_values[:, None] * bin_values[None, :], TS).astype(jnp.float32) * (2.0 * math.pi / TS)
    return jnp.concatenate([jnp.cos(phase), -jnp.sin(phase)], axis=1)

def cross_spectrum(source, receiver):
    src_values = source.astype(jnp.float32)
    rcv_values = receiver.astype(jnp.float32)
    src_real = src_values[:, :NF, :, None]
    src_imag = src_values[:, NF:, :, None]
    rcv_real = rcv_values[:, :NF, None, :]
    rcv_imag = rcv_values[:, NF:, None, :]
    real_part = lax.optimization_barrier(jnp.sum(src_real * rcv_real + src_imag * rcv_imag, axis=0))
    imag_part = lax.optimization_barrier(jnp.sum(src_real * rcv_imag - src_imag * rcv_real, axis=0))
    return jnp.concatenate([real_part, imag_part], axis=0)

def band_window(window_samples):
    full_spectrum = jnp.fft.rfft(window_samples, axis=1)[:, F0:F0 + NF, :]
    return whiten(jnp.real(full_spectrum), jnp.imag(full_spectrum))

def reference(recordings, pair_blocks, pair_count):
    whitened = lax.map(band_window, recordings)
    lag_weights = lag_table()
    stride_width = CH // VS
    flat_pairs = pair_blocks.reshape(NB * MAXP, 2)
    live_slots = (jnp.arange(MAXP, dtype=jnp.int32)[None, :] < pair_count[:, None]).reshape(NB * MAXP)

    def one_pair(entry):
        blocks, alive = entry
        source = whitened[:, blocks[0], :, ::stride_width]
        receiver = whitened[:, blocks[1]]
        spectrum = cross_spectrum(source, receiver)
        result = jnp.einsum('lf,fjc->jlc', lag_weights, spectrum, precision=lax.Precision.HIGHEST)
        return jnp.where(alive, result, jnp.zeros_like(result))
    stacks = lax.map(one_pair, (flat_pairs, live_slots))
    stacks = stacks.reshape(NB, MAXP * VS, LAGS, CH)
    return stacks * (1.0 / math.sqrt(NF * WINDOWS))
```

```python
import functools
import math

import jax
import jax.numpy as jnp
import numpy as np
from jax import lax
from jax.experimental import pallas as pl
from jax.experimental.pallas import tpu as pltpu
from jax.sharding import PartitionSpec as P

TS = 6000
F0 = 60
NF = 1152
MAXLAG = 200
LAGS = 401
VS = 2
REACH = 4
MAXP = 4
EPSILON = 1e-06

QN = 75
PN = 80
KN = 38
KPAD = 40
QPAD = 80
SLOT = 32
GROUP = 2 * SLOT
FN = KN * GROUP
CHUNKS = FN // 128
SRC = 24
TAIL = 2 * SRC
ROWS = FN + TAIL
TABLE = FN + 2 * SRC - 1
HALF = 96
RANK = 2 * HALF
STEP = 16
BF = jnp.bfloat16
F32 = jnp.float32


def cos_table():
    index = np.arange(TS)
    folded = np.minimum(index, TS - index)
    sign = np.where(folded > TS // 4, -1.0, 1.0)
    folded = np.where(folded > TS // 4, TS // 2 - folded, folded)
    square = (folded * (2.0 * math.pi / TS)) ** 2
    value = np.ones(TS)
    for order in range(28, 0, -2):
        value = 1.0 - value * square / (order * (order - 1.0))
    return sign * value


COS = cos_table()


def cosine(index):
    return COS[np.mod(index, TS)]


def sine(index):
    return COS[np.mod(index - TS // 4, TS)]


def split(table):
    high = np.asarray(table, np.float32).astype(BF)
    low = (table - high.astype(np.float64)).astype(np.float32).astype(BF)
    return high, low


def bin_slots():
    bins = np.full((KN, SLOT), -1, np.int64)
    flipped = np.zeros((KN, SLOT), bool)
    for residue in range(KN):
        found = [(k, False) for k in range(F0, F0 + NF) if k % QN == residue]
        if residue:
            found += [(k, True) for k in range(F0, F0 + NF) if k % QN == QN - residue]
        for slot, (k, conj) in enumerate(found):
            bins[residue, slot] = k
            flipped[residue, slot] = conj
    return bins, flipped


def first_matrix():
    residue = np.arange(KN)[:, None]
    q = np.arange(QN)[None, :]
    weights = np.zeros((2 * KPAD, QPAD))
    weights[:KN, :QN] = cosine(PN * residue * q)
    weights[KPAD : KPAD + KN, :QN] = -sine(PN * residue * q)
    high, low = split(weights)
    zero = np.zeros_like(low)
    return np.concatenate(
        [np.concatenate([high, high], 1), np.concatenate([low, zero], 1)], 0
    )


def second_matrix():
    bins, flipped = bin_slots()
    p = np.arange(PN)
    weights = np.zeros((KN, GROUP, 2 * PN))
    cos = cosine(bins[:, :, None] * p)
    sin = sine(bins[:, :, None] * p)
    sign = np.where(flipped, -1.0, 1.0)[:, :, None]
    live = (bins >= 0).astype(np.float64)[:, :, None]
    weights[:, :SLOT, :PN] = live * cos
    weights[:, :SLOT, PN:] = live * sign * sin
    weights[:, SLOT:, :PN] = -live * sin
    weights[:, SLOT:, PN:] = live * sign * cos
    high, low = split(weights)
    return np.concatenate([high, low], 1)


def basis(table):
    rest = table.copy()
    columns = []
    for _ in range(HALF):
        norms = (rest * rest).sum(0)
        column = rest[:, int(norms.argmax())]
        for _ in range(2):
            for other in columns:
                column = column - other * np.cumsum(other * column)[-1]
        column = column / np.sqrt(np.cumsum(column * column)[-1])
        columns.append(column)
        rest = rest - column[:, None] * (column[:, None] * rest).sum(0)[None]
    return columns


@functools.lru_cache(None)
def lag_factors():
    bins, _ = bin_slots()
    live = (bins >= 0).astype(np.float64)
    lag = np.arange(MAXLAG + 1)[:, None]
    band = np.arange(F0, F0 + NF)[None, :]
    even_table = cosine(lag * band)
    odd_table = sine(lag[1:] * band)
    even = basis(even_table)
    odd = basis(odd_table)
    inner = np.zeros((RANK, KN, 2, SLOT))
    place = np.maximum(bins - F0, 0)
    for i in range(HALF):
        row = (even[i][:, None] * even_table).sum(0)[place] * live
        inner[i, :, 0] = row
        inner[i, :, 1] = row
        row = (odd[i][:, None] * odd_table).sum(0)[place] * live
        inner[HALF + i, :, 0] = -row
        inner[HALF + i, :, 1] = row
    outer = np.zeros((LAGS, RANK))
    for i in range(HALF):
        outer[MAXLAG:, i] = even[i]
        outer[MAXLAG::-1, i] = even[i]
        outer[MAXLAG + 1 :, HALF + i] = -odd[i]
        outer[MAXLAG - 1 :: -1, HALF + i] = odd[i]
    return outer, inner.reshape(RANK, FN).astype(np.float32)


def halves(value):
    high = value.astype(BF)
    low = (value - high.astype(F32)).astype(BF)
    return high, low


def dot(left, right):
    return jnp.dot(left, right, preferred_element_type=F32)


def spectrum_kernel(pairs_ref, count_ref, x_ref, first_ref, second_ref, out_ref, xs, ts, zs, ss):
    step = pl.program_id(0)

    @pl.when(step == 0)
    def _():
        xs[72:80, :] = jnp.zeros((8, xs.shape[1]), F32)

    flat = x_ref.reshape(QN * STEP, 128)
    for s in range(STEP):
        xs[0:QN, s * 128 : (s + 1) * 128] = flat[pl.ds(s, QN, stride=STEP), :]
    for pair in range(STEP // 2):
        high, low = halves(xs[:, pair * 256 : (pair + 1) * 256])
        both = dot(first_ref[...], jnp.concatenate([high, low], 0))
        section = both[: 2 * KPAD] + both[2 * KPAD :]
        for side in range(2):
            p = step * STEP + pair * 2 + side
            part = section[:, side * 128 : (side + 1) * 128]
            ts[pl.ds(p, KPAD, stride=2 * PN), :] = part[:KPAD]
            ts[pl.ds(PN + p, KPAD, stride=2 * PN), :] = part[KPAD:]

    @pl.when(step == pl.num_programs(0) - 1)
    def _():
        def residue(k, power):
            high, low = halves(ts[pl.ds(pl.multiple_of(k * 2 * PN, 2 * PN), 2 * PN), :])
            product = dot(second_ref[k], jnp.concatenate([high, low], 1))
            value = product[:GROUP, :128] + (product[:GROUP, 128:] + product[GROUP:, :128])
            zs[pl.ds(pl.multiple_of(k * GROUP, GROUP), GROUP), :] = value
            return power + jnp.sum(value * value, axis=0, keepdims=True)

        power = lax.fori_loop(0, KN, residue, jnp.zeros((1, 128), F32), unroll=2)
        factor = lax.rsqrt(power * (1.0 / NF) + EPSILON)
        out_ref[0:FN, :] = (zs[...] * factor).astype(BF)
        lane = lax.broadcasted_iota(jnp.int32, (8, 128), 1)
        sub = lax.broadcasted_iota(jnp.int32, (8, 128), 0)
        pick = jnp.where(lane == sub * (128 // VS), 1.0, 0.0).astype(BF)
        rows = lax.dot_general(
            pick, out_ref[0:FN, :], (((1,), (1,)), ((), ())), preferred_element_type=F32
        )
        ss[...] = jnp.zeros_like(ss)
        for j in range(VS):
            for c in range(CHUNKS):
                ss[j * SRC + c : j * SRC + c + 1, :] = rows[j : j + 1, c * 128 : (c + 1) * 128]
        owner = lax.axis_index("fibre")
        lane = lax.broadcasted_iota(jnp.int32, (1, 128), 1)
        table = jnp.where(lane == 2 * MAXP, count_ref[0], 0)
        for slot in range(MAXP):
            for side in range(2):
                offset = pairs_ref[slot * 2 + side] - owner
                table = jnp.where(lane == slot * 2 + side, offset, table)
        ss[TABLE - FN : TABLE - FN + 1, :] = table.astype(F32)
        out_ref[FN:ROWS, :] = ss[...].astype(BF)


def spectra(pair_blocks, pair_count, samples):
    smem = pl.BlockSpec(memory_space=pltpu.SMEM)
    first = jnp.asarray(first_matrix())
    second = jnp.asarray(second_matrix())
    return pl.pallas_call(
        spectrum_kernel,
        grid=(PN // STEP,),
        in_specs=[
            smem,
            smem,
            pl.BlockSpec((QN, STEP, 128), lambda g: (0, g, 0)),
            pl.BlockSpec(first.shape, lambda g: (0, 0)),
            pl.BlockSpec(second.shape, lambda g: (0, 0, 0)),
        ],
        out_specs=pl.BlockSpec((ROWS, 128), lambda g: (0, 0)),
        out_shape=jax.ShapeDtypeStruct((ROWS, 128), BF),
        scratch_shapes=[
            pltpu.VMEM((QPAD, STEP * 128), F32),
            pltpu.VMEM((KPAD * 2 * PN, 128), F32),
            pltpu.VMEM((FN, 128), F32),
            pltpu.VMEM((TAIL, 128), F32),
        ],
        compiler_params=pltpu.CompilerParams(vmem_limit_bytes=28 * 2**20),
        name="spectra",
    )(pair_blocks, pair_count, samples, first, second)


def pairs_kernel(b0, b1, b2, b3, b4, inner_ref, out_ref, receiver, source, weights):
    blocks = (b0, b1, b2, b3, b4)
    tail = b0[FN:ROWS, :].astype(F32)
    row = tail[TABLE - FN : TABLE - FN + 1, :].astype(jnp.int32)
    lane = lax.broadcasted_iota(jnp.int32, (1, 128), 1)

    def entry(index):
        return jnp.sum(jnp.where(lane == index, row, 0))

    count = entry(2 * MAXP)
    spot = lax.broadcasted_iota(jnp.int32, (TAIL, 128), 1)
    real_spot = lax.rem(spot, GROUP) < SLOT

    def one_pair(slot, carry):
        first = entry(2 * slot)
        second = entry(2 * slot + 1)
        for place, block in enumerate(blocks):

            @pl.when(second == place)
            def _():
                receiver[...] = block[0:FN, :]

            @pl.when(first == place)
            def _():
                source[...] = block[FN:ROWS, :].astype(F32)

        straight = source[...]
        crossed = jnp.where(
            real_spot, pltpu.roll(straight, 128 - SLOT, 1), pltpu.roll(straight, SLOT, 1)
        )
        for j in range(VS):
            for c in range(CHUNKS):
                at = j * SRC + c
                here = pl.ds(c * 128, 128)
                even = inner_ref[0:HALF, here] * straight[at : at + 1, :]
                odd = inner_ref[HALF:RANK, here] * crossed[at : at + 1, :]
                weights[j * RANK : j * RANK + HALF, here] = even.astype(BF)
                weights[j * RANK + HALF : (j + 1) * RANK, here] = odd.astype(BF)
        result = dot(weights[...], receiver[...]).astype(BF)
        for j in range(VS):
            out_ref[slot * VS + j] = result[j * RANK : (j + 1) * RANK]
        return carry

    def one_blank(slot, carry):
        for j in range(VS):
            out_ref[slot * VS + j] = jnp.zeros((RANK, 128), BF)
        return carry

    lax.fori_loop(0, count, one_pair, 0)
    lax.fori_loop(count, MAXP, one_blank, 0)


def pair_rows(blocks):
    _, inner = lag_factors()
    vmem = pl.BlockSpec(memory_space=pltpu.VMEM)
    return pl.pallas_call(
        pairs_kernel,
        in_specs=[vmem] * 6,
        out_specs=vmem,
        out_shape=jax.ShapeDtypeStruct((MAXP * VS, RANK, 128), BF),
        scratch_shapes=[
            pltpu.VMEM((FN, 128), BF),
            pltpu.VMEM((TAIL, 128), F32),
            pltpu.VMEM((VS * RANK, FN), BF),
        ],
        compiler_params=pltpu.CompilerParams(vmem_limit_bytes=28 * 2**20),
        name="pair_rows",
    )(*blocks, jnp.asarray(inner))


def lags_kernel(row_ref, outer_ref, out_ref):
    high, low = halves(row_ref[...])
    out_ref[...] = dot(outer_ref[...], jnp.concatenate([high, low, high], 0))


def lag_rows(row):
    outer, _ = lag_factors()
    high, low = split(outer * (1.0 / math.sqrt(NF * 8)))
    table = jnp.asarray(np.concatenate([high, high, low], 1))
    vmem = pl.BlockSpec(memory_space=pltpu.VMEM)
    return pl.pallas_call(
        lags_kernel,
        in_specs=[vmem, vmem],
        out_specs=vmem,
        out_shape=jax.ShapeDtypeStruct((LAGS, 128), F32),
        name="lag_rows",
    )(row, table)


def turned(array, by):
    size = lax.axis_size("fibre")
    return lax.ppermute(array, "fibre", [(i, (i + by) % size) for i in range(size)])


def shards(recordings, pair_blocks, pair_count):
    samples = recordings.reshape(QN, PN, 128)
    own = spectra(pair_blocks.reshape(2 * MAXP), pair_count, samples)
    middle = REACH // 2
    blocks = [own if d == middle else turned(own, middle - d) for d in range(REACH + 1)]
    rows = pair_rows(blocks)
    shared = lax.all_to_all(rows, "tm", 0, 0)
    row = jnp.sum(shared.astype(F32), axis=0)
    return lag_rows(turned(row, -middle))[None, None]


def solution(mesh):
    in_specs = (P("tm", "fibre", None, None), P("fibre", None, None), P("fibre"))
    out_specs = P("fibre", "tm", None, None)
    return jax.shard_map(shards, mesh=mesh, in_specs=in_specs, out_specs=out_specs, check_vma=False)
```

```python
import functools
import math

import jax
import jax.numpy as jnp
import numpy as np
from jax import lax
from jax.experimental import pallas as pl
from jax.experimental.pallas import tpu as pltpu
from jax.sharding import PartitionSpec as P

TS = 6000
F0 = 60
NF = 1152
MAXLAG = 200
LAGS = 401
VS = 2
REACH = 4
MAXP = 4
EPSILON = 1e-06

QN = 75
PN = 80
KN = 38
KPAD = 40
QPAD = 80
SLOT = 32
GROUP = 2 * SLOT
FN = KN * GROUP
CHUNKS = FN // 128
SRC = 24
TAIL = 2 * SRC
ROWS = FN + TAIL
TABLE = FN + 2 * SRC - 1
HALF = 96
RANK = 2 * HALF
STEP = 16
STEPS = PN // STEP
UNROLL = 19
FRONT_VMEM = 28 * 2**20
BF = jnp.bfloat16
F32 = jnp.float32


def cos_table():
    index = np.arange(TS)
    folded = np.minimum(index, TS - index)
    sign = np.where(folded > TS // 4, -1.0, 1.0)
    folded = np.where(folded > TS // 4, TS // 2 - folded, folded)
    square = (folded * (2.0 * math.pi / TS)) ** 2
    value = np.ones(TS)
    for order in range(28, 0, -2):
        value = 1.0 - value * square / (order * (order - 1.0))
    return sign * value


COS = cos_table()


def cosine(index):
    return COS[np.mod(index, TS)]


def sine(index):
    return COS[np.mod(index - TS // 4, TS)]


def split(table):
    high = np.asarray(table, np.float32).astype(BF)
    low = (table - high.astype(np.float64)).astype(np.float32).astype(BF)
    return high, low


def bin_slots():
    bins = np.full((KN, SLOT), -1, np.int64)
    flipped = np.zeros((KN, SLOT), bool)
    for residue in range(KN):
        found = [(k, False) for k in range(F0, F0 + NF) if k % QN == residue]
        if residue:
            found += [(k, True) for k in range(F0, F0 + NF) if k % QN == QN - residue]
        for slot, (k, conj) in enumerate(found):
            bins[residue, slot] = k
            flipped[residue, slot] = conj
    return bins, flipped


def first_matrix():
    residue = np.arange(KN)[:, None]
    q = np.arange(QN)[None, :]
    weights = np.zeros((2 * KPAD, QPAD))
    weights[:KN, :QN] = cosine(PN * residue * q)
    weights[KPAD : KPAD + KN, :QN] = -sine(PN * residue * q)
    high, low = split(weights)
    zero = np.zeros_like(low)
    return np.concatenate(
        [np.concatenate([high, high], 1), np.concatenate([low, zero], 1)], 0
    )


def second_matrix():
    bins, flipped = bin_slots()
    p = np.arange(PN)
    weights = np.zeros((KN, GROUP, 2 * PN))
    cos = cosine(bins[:, :, None] * p)
    sin = sine(bins[:, :, None] * p)
    sign = np.where(flipped, -1.0, 1.0)[:, :, None]
    live = (bins >= 0).astype(np.float64)[:, :, None]
    weights[:, :SLOT, :PN] = live * cos
    weights[:, :SLOT, PN:] = live * sign * sin
    weights[:, SLOT:, :PN] = -live * sin
    weights[:, SLOT:, PN:] = live * sign * cos
    high, low = split(weights)
    return np.concatenate([high, low], 1)


def basis(table):
    rest = table.copy()
    columns = []
    for _ in range(HALF):
        norms = (rest * rest).sum(0)
        column = rest[:, int(norms.argmax())]
        for _ in range(2):
            for other in columns:
                column = column - other * np.cumsum(other * column)[-1]
        column = column / np.sqrt(np.cumsum(column * column)[-1])
        columns.append(column)
        rest = rest - column[:, None] * (column[:, None] * rest).sum(0)[None]
    return columns


@functools.lru_cache(None)
def lag_factors():
    bins, _ = bin_slots()
    live = (bins >= 0).astype(np.float64)
    lag = np.arange(MAXLAG + 1)[:, None]
    band = np.arange(F0, F0 + NF)[None, :]
    even_table = cosine(lag * band)
    odd_table = sine(lag[1:] * band)
    even = basis(even_table)
    odd = basis(odd_table)
    inner = np.zeros((RANK, KN, 2, SLOT))
    place = np.maximum(bins - F0, 0)
    for i in range(HALF):
        row = (even[i][:, None] * even_table).sum(0)[place] * live
        inner[i, :, 0] = row
        inner[i, :, 1] = row
        row = (odd[i][:, None] * odd_table).sum(0)[place] * live
        inner[HALF + i, :, 0] = -row
        inner[HALF + i, :, 1] = row
    outer = np.zeros((LAGS, RANK))
    for i in range(HALF):
        outer[MAXLAG:, i] = even[i]
        outer[MAXLAG::-1, i] = even[i]
        outer[MAXLAG + 1 :, HALF + i] = -odd[i]
        outer[MAXLAG - 1 :: -1, HALF + i] = odd[i]
    return outer, inner.reshape(RANK, FN).astype(np.float32)


def halves(value):
    high = value.astype(BF)
    low = (value - high.astype(F32)).astype(BF)
    return high, low


def dot(left, right):
    return jnp.dot(left, right, preferred_element_type=F32)


def spectrum_kernel(
    pairs_ref, count_ref, x_hbm, first_hbm, second_hbm, out_ref,
    xs, first, second, pad, ts, zs, ss, sems,
):
    def load(g):
        return pltpu.make_async_copy(
            x_hbm.at[:, pl.ds(g * STEP, STEP), :], xs.at[g], sems.at[g]
        )

    first_copy = pltpu.make_async_copy(first_hbm, first, sems.at[STEPS])
    second_copy = pltpu.make_async_copy(second_hbm, second, sems.at[STEPS + 1])
    first_copy.start()
    for g in range(STEPS):
        load(g).start()
    second_copy.start()
    pad[72:80, :] = jnp.zeros((8, STEP * 128), F32)

    def sections(g, carry):
        load(g).wait()
        flat = xs.at[g].reshape(QN * STEP, 128)
        for s in range(STEP):
            pad[0:QN, s * 128 : (s + 1) * 128] = flat[pl.ds(s, QN, stride=STEP), :]
        for pair in range(STEP // 2):
            high, low = halves(pad[:, pair * 256 : (pair + 1) * 256])
            both = dot(first[...], jnp.concatenate([high, low], 0))
            section = both[: 2 * KPAD] + both[2 * KPAD :]
            for side in range(2):
                p = g * STEP + pair * 2 + side
                part = section[:, side * 128 : (side + 1) * 128]
                ts[pl.ds(p, KPAD, stride=2 * PN), :] = part[:KPAD]
                ts[pl.ds(PN + p, KPAD, stride=2 * PN), :] = part[KPAD:]
        return carry

    first_copy.wait()
    lax.fori_loop(0, STEPS, sections, 0)
    second_copy.wait()

    def residue(k, power):
        high, low = halves(ts[pl.ds(pl.multiple_of(k * 2 * PN, 2 * PN), 2 * PN), :])
        product = dot(second[k], jnp.concatenate([high, low], 1))
        value = product[:GROUP, :128] + (product[:GROUP, 128:] + product[GROUP:, :128])
        zs[pl.ds(pl.multiple_of(k * GROUP, GROUP), GROUP), :] = value
        return power + jnp.sum((value * value).reshape(GROUP // 8, 8, 128), axis=0)

    power = lax.fori_loop(0, KN, residue, jnp.zeros((8, 128), F32), unroll=UNROLL)
    power = jnp.sum(power, axis=0, keepdims=True)
    factor = lax.rsqrt(power * (1.0 / NF) + EPSILON)
    out_ref[0:FN, :] = (zs[...] * factor).astype(BF)
    lane = lax.broadcasted_iota(jnp.int32, (8, 128), 1)
    sub = lax.broadcasted_iota(jnp.int32, (8, 128), 0)
    pick = jnp.where(lane == sub * (128 // VS), 1.0, 0.0).astype(BF)
    rows = lax.dot_general(
        pick, out_ref[0:FN, :], (((1,), (1,)), ((), ())), preferred_element_type=F32
    )
    ss[...] = jnp.zeros_like(ss)
    for j in range(VS):
        for c in range(CHUNKS):
            ss[j * SRC + c : j * SRC + c + 1, :] = rows[j : j + 1, c * 128 : (c + 1) * 128]
    owner = lax.axis_index("fibre")
    lane = lax.broadcasted_iota(jnp.int32, (1, 128), 1)
    table = jnp.where(lane == 2 * MAXP, count_ref[0], 0)
    for slot in range(MAXP):
        for side in range(2):
            offset = pairs_ref[side, slot] - owner
            table = jnp.where(lane == slot * 2 + side, offset, table)
    ss[TABLE - FN : TABLE - FN + 1, :] = table.astype(F32)
    out_ref[FN:ROWS, :] = ss[...].astype(BF)


def in_hbm(array):
    return pltpu.with_memory_space_constraint(array, pltpu.HBM)


def spectra(pair_blocks, pair_count, samples):
    smem = pl.BlockSpec(memory_space=pltpu.SMEM)
    vmem = pl.BlockSpec(memory_space=pltpu.VMEM)
    hbm = pl.BlockSpec(memory_space=pltpu.HBM)
    first = jnp.asarray(first_matrix())
    second = jnp.asarray(second_matrix())
    return pl.pallas_call(
        spectrum_kernel,
        in_specs=[smem, smem, hbm, hbm, hbm],
        out_specs=vmem,
        out_shape=jax.ShapeDtypeStruct((ROWS, 128), BF),
        scratch_shapes=[
            pltpu.VMEM((STEPS, QN, STEP, 128), F32),
            pltpu.VMEM(first.shape, BF),
            pltpu.VMEM(second.shape, BF),
            pltpu.VMEM((QPAD, STEP * 128), F32),
            pltpu.VMEM((KPAD * 2 * PN, 128), F32),
            pltpu.VMEM((FN, 128), F32),
            pltpu.VMEM((TAIL, 128), F32),
            pltpu.SemaphoreType.DMA((STEPS + 2,)),
        ],
        compiler_params=pltpu.CompilerParams(vmem_limit_bytes=FRONT_VMEM),
        name="spectra",
    )(
        in_hbm(pair_blocks), pair_count, in_hbm(samples), in_hbm(first), in_hbm(second)
    )


def pairs_kernel(b0, b1, b2, b3, b4, inner_ref, out_ref, receiver, source, weights):
    blocks = (b0, b1, b2, b3, b4)
    tail = b0[FN:ROWS, :].astype(F32)
    row = tail[TABLE - FN : TABLE - FN + 1, :].astype(jnp.int32)
    lane = lax.broadcasted_iota(jnp.int32, (1, 128), 1)

    def entry(index):
        return jnp.sum(jnp.where(lane == index, row, 0))

    even = lax.rem(lax.axis_index("fibre"), 2) == 0

    def place_of(offset):
        return jnp.where(even & (lax.rem(offset, 2) == 1), REACH - offset, offset)

    count = entry(2 * MAXP)
    spot = lax.broadcasted_iota(jnp.int32, (TAIL, 128), 1)
    real_spot = lax.rem(spot, GROUP) < SLOT

    def one_pair(slot, carry):
        first = place_of(entry(2 * slot))
        second = place_of(entry(2 * slot + 1))
        for place, block in enumerate(blocks):

            @pl.when(second == place)
            def _():
                receiver[...] = block[0:FN, :]

            @pl.when(first == place)
            def _():
                source[...] = block[FN:ROWS, :].astype(F32)

        straight = source[...]
        crossed = jnp.where(
            real_spot, pltpu.roll(straight, 128 - SLOT, 1), pltpu.roll(straight, SLOT, 1)
        )
        for j in range(VS):
            for c in range(CHUNKS):
                at = j * SRC + c
                here = pl.ds(c * 128, 128)
                even = inner_ref[0:HALF, here] * straight[at : at + 1, :]
                odd = inner_ref[HALF:RANK, here] * crossed[at : at + 1, :]
                weights[j * RANK : j * RANK + HALF, here] = even.astype(BF)
                weights[j * RANK + HALF : (j + 1) * RANK, here] = odd.astype(BF)
        result = dot(weights[...], receiver[...]).astype(BF)
        for j in range(VS):
            out_ref[slot * VS + j] = result[j * RANK : (j + 1) * RANK]
        return carry

    def one_blank(slot, carry):
        for j in range(VS):
            out_ref[slot * VS + j] = jnp.zeros((RANK, 128), BF)
        return carry

    lax.fori_loop(0, count, one_pair, 0)
    lax.fori_loop(count, MAXP, one_blank, 0)


def pair_rows(blocks):
    _, inner = lag_factors()
    vmem = pl.BlockSpec(memory_space=pltpu.VMEM)
    return pl.pallas_call(
        pairs_kernel,
        in_specs=[vmem] * 6,
        out_specs=vmem,
        out_shape=jax.ShapeDtypeStruct((MAXP * VS, RANK, 128), BF),
        scratch_shapes=[
            pltpu.VMEM((FN, 128), BF),
            pltpu.VMEM((TAIL, 128), F32),
            pltpu.VMEM((VS * RANK, FN), BF),
        ],
        compiler_params=pltpu.CompilerParams(vmem_limit_bytes=28 * 2**20),
        name="pair_rows",
    )(*blocks, jnp.asarray(inner))


def lags_kernel(row_ref, outer_ref, out_ref):
    high, low = halves(row_ref[...])
    out_ref[:, 0, :] = dot(outer_ref[...], jnp.concatenate([high, low, high], 0))


def lag_rows(row):
    outer, _ = lag_factors()
    high, low = split(outer * (1.0 / math.sqrt(NF * 8)))
    table = jnp.asarray(np.concatenate([high, high, low], 1))
    vmem = pl.BlockSpec(memory_space=pltpu.VMEM)
    return pl.pallas_call(
        lags_kernel,
        in_specs=[vmem, vmem],
        out_specs=vmem,
        out_shape=jax.ShapeDtypeStruct((LAGS, 1, 128), F32),
        compiler_params=pltpu.CompilerParams(vmem_limit_bytes=8 * 2**20),
        name="lag_rows",
    )(row, table)


def turned(array, by):
    size = lax.axis_size("fibre")
    return lax.ppermute(array, "fibre", [(i, (i + by) % size) for i in range(size)])


def swapped(array):
    size = lax.axis_size("fibre")
    return lax.ppermute(array, "fibre", [(i, i ^ 1) for i in range(size)])


def gathered(own):
    even = lax.axis_index("fibre") % 2 == 0
    ahead = turned(own, -2)
    behind = turned(own, 2)
    sibling = swapped(own)
    other = swapped(jnp.where(even, ahead, behind))
    return [behind, sibling, own, other, ahead]


def shards(recordings, pair_blocks, pair_count):
    samples = recordings.reshape(QN, PN, 128)
    own = spectra(pair_blocks[0].T, pair_count, samples)
    rows = pair_rows(gathered(own))
    shared = lax.all_to_all(rows, "tm", 0, 0)
    row = jnp.sum(shared.astype(F32), axis=0)
    return lag_rows(turned(row, -2))[None].transpose(0, 2, 1, 3)


def solution(mesh):
    in_specs = (P("tm", "fibre", None, None), P("fibre", None, None), P("fibre"))
    out_specs = P("fibre", "tm", None, None)
    return jax.shard_map(shards, mesh=mesh, in_specs=in_specs, out_specs=out_specs, check_vma=False)
```

```python
import functools
import math

import jax
import jax.numpy as jnp
import numpy as np
from jax import lax
from jax.experimental import pallas as pl
from jax.experimental.pallas import tpu as pltpu
from jax.sharding import PartitionSpec as P

TS = 6000
F0 = 60
NF = 1152
MAXLAG = 200
LAGS = 401
VS = 2
REACH = 4
MAXP = 4
EPSILON = 1e-06

QN = 75
PN = 80
KN = 38
KPAD = 40
QPAD = 80
SLOT = 32
GROUP = 2 * SLOT
FN = KN * GROUP
CHUNKS = FN // 128
SRC = 24
TAIL = 2 * SRC
ROWS = FN + TAIL
HALF = 96
RANK = 2 * HALF
STEP = 16
STEPS = PN // STEP
UNROLL = 19
FRONT_VMEM = 28 * 2**20
BF = jnp.bfloat16
F32 = jnp.float32


def cos_table():
    index = np.arange(TS)
    folded = np.minimum(index, TS - index)
    sign = np.where(folded > TS // 4, -1.0, 1.0)
    folded = np.where(folded > TS // 4, TS // 2 - folded, folded)
    square = (folded * (2.0 * math.pi / TS)) ** 2
    value = np.ones(TS)
    for order in range(28, 0, -2):
        value = 1.0 - value * square / (order * (order - 1.0))
    return sign * value


COS = cos_table()


def cosine(index):
    return COS[np.mod(index, TS)]


def sine(index):
    return COS[np.mod(index - TS // 4, TS)]


def split(table):
    high = np.asarray(table, np.float32).astype(BF)
    low = (table - high.astype(np.float64)).astype(np.float32).astype(BF)
    return high, low


def bin_slots():
    bins = np.full((KN, SLOT), -1, np.int64)
    flipped = np.zeros((KN, SLOT), bool)
    for residue in range(KN):
        found = [(k, False) for k in range(F0, F0 + NF) if k % QN == residue]
        if residue:
            found += [(k, True) for k in range(F0, F0 + NF) if k % QN == QN - residue]
        for slot, (k, conj) in enumerate(found):
            bins[residue, slot] = k
            flipped[residue, slot] = conj
    return bins, flipped


def first_matrix():
    residue = np.arange(KN)[:, None]
    q = np.arange(QN)[None, :]
    weights = np.zeros((2 * KPAD, QPAD))
    weights[:KN, :QN] = cosine(PN * residue * q)
    weights[KPAD : KPAD + KN, :QN] = -sine(PN * residue * q)
    high, low = split(weights)
    zero = np.zeros_like(low)
    return np.concatenate(
        [np.concatenate([high, high], 1), np.concatenate([low, zero], 1)], 0
    )


def second_matrix():
    bins, flipped = bin_slots()
    p = np.arange(PN)
    weights = np.zeros((KN, GROUP, 2 * PN))
    cos = cosine(bins[:, :, None] * p)
    sin = sine(bins[:, :, None] * p)
    sign = np.where(flipped, -1.0, 1.0)[:, :, None]
    live = (bins >= 0).astype(np.float64)[:, :, None]
    weights[:, :SLOT, :PN] = live * cos
    weights[:, :SLOT, PN:] = live * sign * sin
    weights[:, SLOT:, :PN] = -live * sin
    weights[:, SLOT:, PN:] = live * sign * cos
    high, low = split(weights)
    return np.concatenate([high, low], 1)


def basis(table):
    rest = table.copy()
    columns = []
    for _ in range(HALF):
        norms = (rest * rest).sum(0)
        column = rest[:, int(norms.argmax())]
        for _ in range(2):
            for other in columns:
                column = column - other * np.cumsum(other * column)[-1]
        column = column / np.sqrt(np.cumsum(column * column)[-1])
        columns.append(column)
        rest = rest - column[:, None] * (column[:, None] * rest).sum(0)[None]
    return columns


@functools.lru_cache(None)
def lag_factors():
    bins, _ = bin_slots()
    live = (bins >= 0).astype(np.float64)
    lag = np.arange(MAXLAG + 1)[:, None]
    band = np.arange(F0, F0 + NF)[None, :]
    even_table = cosine(lag * band)
    odd_table = sine(lag[1:] * band)
    even = basis(even_table)
    odd = basis(odd_table)
    inner = np.zeros((RANK, KN, 2, SLOT))
    place = np.maximum(bins - F0, 0)
    for i in range(HALF):
        row = (even[i][:, None] * even_table).sum(0)[place] * live
        inner[i, :, 0] = row
        inner[i, :, 1] = row
        row = (odd[i][:, None] * odd_table).sum(0)[place] * live
        inner[HALF + i, :, 0] = -row
        inner[HALF + i, :, 1] = row
    outer = np.zeros((LAGS, RANK))
    for i in range(HALF):
        outer[MAXLAG:, i] = even[i]
        outer[MAXLAG::-1, i] = even[i]
        outer[MAXLAG + 1 :, HALF + i] = -odd[i]
        outer[MAXLAG - 1 :: -1, HALF + i] = odd[i]
    return outer, inner.reshape(RANK, FN).astype(np.float32)


def halves(value):
    high = value.astype(BF)
    low = (value - high.astype(F32)).astype(BF)
    return high, low


def dot(left, right):
    return jnp.dot(left, right, preferred_element_type=F32)


def spectrum_kernel(
    x_hbm, first_hbm, second_hbm, out_ref, xs, first, second, pad, ts, zs, ss, sems
):
    def load(g):
        return pltpu.make_async_copy(
            x_hbm.at[:, pl.ds(g * STEP, STEP), :], xs.at[g], sems.at[g]
        )

    first_copy = pltpu.make_async_copy(first_hbm, first, sems.at[STEPS])
    second_copy = pltpu.make_async_copy(second_hbm, second, sems.at[STEPS + 1])
    first_copy.start()
    for g in range(STEPS):
        load(g).start()
    second_copy.start()
    pad[72:80, :] = jnp.zeros((8, STEP * 128), F32)

    def sections(g, carry):
        load(g).wait()
        flat = xs.at[g].reshape(QN * STEP, 128)
        for s in range(STEP):
            pad[0:QN, s * 128 : (s + 1) * 128] = flat[pl.ds(s, QN, stride=STEP), :]
        for pair in range(STEP // 2):
            high, low = halves(pad[:, pair * 256 : (pair + 1) * 256])
            both = dot(first[...], jnp.concatenate([high, low], 0))
            section = both[: 2 * KPAD] + both[2 * KPAD :]
            for side in range(2):
                p = g * STEP + pair * 2 + side
                part = section[:, side * 128 : (side + 1) * 128]
                ts[pl.ds(p, KPAD, stride=2 * PN), :] = part[:KPAD]
                ts[pl.ds(PN + p, KPAD, stride=2 * PN), :] = part[KPAD:]
        return carry

    first_copy.wait()
    lax.fori_loop(0, STEPS, sections, 0)
    second_copy.wait()

    def residue(k, power):
        high, low = halves(ts[pl.ds(pl.multiple_of(k * 2 * PN, 2 * PN), 2 * PN), :])
        product = dot(second[k], jnp.concatenate([high, low], 1))
        value = product[:GROUP, :128] + (product[:GROUP, 128:] + product[GROUP:, :128])
        zs[pl.ds(pl.multiple_of(k * GROUP, GROUP), GROUP), :] = value
        return power + jnp.sum((value * value).reshape(GROUP // 8, 8, 128), axis=0)

    power = lax.fori_loop(0, KN, residue, jnp.zeros((8, 128), F32), unroll=UNROLL)
    power = jnp.sum(power, axis=0, keepdims=True)
    factor = lax.rsqrt(power * (1.0 / NF) + EPSILON)
    out_ref[0:FN, :] = (zs[...] * factor).astype(BF)
    lane = lax.broadcasted_iota(jnp.int32, (8, 128), 1)
    sub = lax.broadcasted_iota(jnp.int32, (8, 128), 0)
    pick = jnp.where(lane == sub * (128 // VS), 1.0, 0.0).astype(BF)
    rows = lax.dot_general(
        pick, out_ref[0:FN, :], (((1,), (1,)), ((), ())), preferred_element_type=F32
    )
    ss[...] = jnp.zeros_like(ss)
    for j in range(VS):
        for c in range(CHUNKS):
            ss[j * SRC + c : j * SRC + c + 1, :] = rows[j : j + 1, c * 128 : (c + 1) * 128]
    out_ref[FN:ROWS, :] = ss[...].astype(BF)


def in_hbm(array):
    return pltpu.with_memory_space_constraint(array, pltpu.HBM)


def spectra(samples):
    vmem = pl.BlockSpec(memory_space=pltpu.VMEM)
    hbm = pl.BlockSpec(memory_space=pltpu.HBM)
    first = jnp.asarray(first_matrix())
    second = jnp.asarray(second_matrix())
    return pl.pallas_call(
        spectrum_kernel,
        in_specs=[hbm, hbm, hbm],
        out_specs=vmem,
        out_shape=jax.ShapeDtypeStruct((ROWS, 128), BF),
        scratch_shapes=[
            pltpu.VMEM((STEPS, QN, STEP, 128), F32),
            pltpu.VMEM(first.shape, BF),
            pltpu.VMEM(second.shape, BF),
            pltpu.VMEM((QPAD, STEP * 128), F32),
            pltpu.VMEM((KPAD * 2 * PN, 128), F32),
            pltpu.VMEM((FN, 128), F32),
            pltpu.VMEM((TAIL, 128), F32),
            pltpu.SemaphoreType.DMA((STEPS + 2,)),
        ],
        compiler_params=pltpu.CompilerParams(vmem_limit_bytes=FRONT_VMEM),
        name="spectra",
    )(in_hbm(samples), in_hbm(first), in_hbm(second))


def pairs_kernel(pairs_ref, count_ref, b0, b1, b2, b3, b4, inner_ref, out_ref, receiver, source, weights):
    blocks = (b0, b1, b2, b3, b4)
    owner = lax.axis_index("fibre")
    odd = lax.rem(owner, 2) == 1

    def place_of(slot, side):
        offset = pairs_ref[side, slot] - owner
        return jnp.where(odd & (lax.rem(offset, 2) == 1), REACH - offset, offset)

    count = count_ref[0]
    spot = lax.broadcasted_iota(jnp.int32, (TAIL, 128), 1)
    real_spot = lax.rem(spot, GROUP) < SLOT

    def one_pair(slot, carry):
        first = place_of(slot, 0)
        second = place_of(slot, 1)
        for place, block in enumerate(blocks):

            @pl.when(second == place)
            def _():
                receiver[...] = block[0:FN, :]

            @pl.when(first == place)
            def _():
                source[...] = block[FN:ROWS, :].astype(F32)

        straight = source[...]
        crossed = jnp.where(
            real_spot, pltpu.roll(straight, 128 - SLOT, 1), pltpu.roll(straight, SLOT, 1)
        )
        for j in range(VS):
            for c in range(CHUNKS):
                at = j * SRC + c
                here = pl.ds(c * 128, 128)
                even = inner_ref[0:HALF, here] * straight[at : at + 1, :]
                odd = inner_ref[HALF:RANK, here] * crossed[at : at + 1, :]
                weights[j * RANK : j * RANK + HALF, here] = even.astype(BF)
                weights[j * RANK + HALF : (j + 1) * RANK, here] = odd.astype(BF)
        result = dot(weights[...], receiver[...]).astype(BF)
        for j in range(VS):
            out_ref[slot * VS + j] = result[j * RANK : (j + 1) * RANK]
        return carry

    def one_blank(slot, carry):
        for j in range(VS):
            out_ref[slot * VS + j] = jnp.zeros((RANK, 128), BF)
        return carry

    lax.fori_loop(0, count, one_pair, 0)
    lax.fori_loop(count, MAXP, one_blank, 0)


def pair_rows(pair_blocks, pair_count, blocks):
    _, inner = lag_factors()
    smem = pl.BlockSpec(memory_space=pltpu.SMEM)
    vmem = pl.BlockSpec(memory_space=pltpu.VMEM)
    return pl.pallas_call(
        pairs_kernel,
        in_specs=[smem] * 2 + [vmem] * 6,
        out_specs=vmem,
        out_shape=jax.ShapeDtypeStruct((MAXP * VS, RANK, 128), BF),
        scratch_shapes=[
            pltpu.VMEM((FN, 128), BF),
            pltpu.VMEM((TAIL, 128), F32),
            pltpu.VMEM((VS * RANK, FN), BF),
        ],
        compiler_params=pltpu.CompilerParams(vmem_limit_bytes=28 * 2**20),
        name="pair_rows",
    )(pair_blocks, pair_count, *blocks, jnp.asarray(inner))


def lags_kernel(row_ref, outer_ref, out_ref):
    high, low = halves(row_ref[...])
    out_ref[:, 0, :] = dot(outer_ref[...], jnp.concatenate([high, low, high], 0))


def lag_rows(row):
    outer, _ = lag_factors()
    high, low = split(outer * (1.0 / math.sqrt(NF * 8)))
    table = jnp.asarray(np.concatenate([high, high, low], 1))
    vmem = pl.BlockSpec(memory_space=pltpu.VMEM)
    return pl.pallas_call(
        lags_kernel,
        in_specs=[vmem, vmem],
        out_specs=vmem,
        out_shape=jax.ShapeDtypeStruct((LAGS, 1, 128), F32),
        compiler_params=pltpu.CompilerParams(vmem_limit_bytes=8 * 2**20),
        name="lag_rows",
    )(row, table)


def turned(array, by):
    size = lax.axis_size("fibre")
    return lax.ppermute(array, "fibre", [(i, (i + by) % size) for i in range(size)])


def swapped(array):
    size = lax.axis_size("fibre")
    return lax.ppermute(array, "fibre", [(i, i ^ 1) for i in range(size)])


def gathered(own):
    even = lax.rem(lax.axis_index("fibre"), 2) == 0
    near = turned(own, -2)
    far = turned(near, -2)
    three = swapped(near)
    one = swapped(jnp.where(even, far, own))
    return [own, one, near, three, far]


def shards(recordings, pair_blocks, pair_count):
    samples = recordings.reshape(QN, PN, 128)
    own = spectra(samples)
    rows = pair_rows(pair_blocks[0].T, pair_count, gathered(own))
    shared = lax.all_to_all(rows, "tm", 0, 0)
    row = jnp.sum(shared.astype(F32), axis=0)
    return lag_rows(row)[None].transpose(0, 2, 1, 3)


def solution(mesh):
    in_specs = (P("tm", "fibre", None, None), P("fibre", None, None), P("fibre"))
    out_specs = P("fibre", "tm", None, None)
    return jax.shard_map(shards, mesh=mesh, in_specs=in_specs, out_specs=out_specs, check_vma=False)
```

```python
import functools
import math

import jax
import jax.numpy as jnp
import numpy as np
from jax import lax
from jax.experimental import pallas as pl
from jax.experimental.pallas import tpu as pltpu
from jax.sharding import PartitionSpec as P

TS = 6000
F0 = 60
NF = 1152
MAXLAG = 200
LAGS = 401
VS = 2
REACH = 4
MAXP = 4
EPSILON = 1e-06

QN = 75
PN = 80
KN = 38
KPAD = 40
QPAD = 80
SLOT = 32
GROUP = 2 * SLOT
FN = KN * GROUP
CHUNKS = FN // 128
SRC = 24
TAIL = 2 * SRC
ROWS = FN + TAIL
TABLE = FN + 2 * SRC - 1
HALF = 96
RANK = 2 * HALF
STEP = 16
STEPS = PN // STEP
UNROLL = 19
FRONT_VMEM = 28 * 2**20
BF = jnp.bfloat16
F32 = jnp.float32


def cos_table():
    index = np.arange(TS)
    folded = np.minimum(index, TS - index)
    sign = np.where(folded > TS // 4, -1.0, 1.0)
    folded = np.where(folded > TS // 4, TS // 2 - folded, folded)
    square = (folded * (2.0 * math.pi / TS)) ** 2
    value = np.ones(TS)
    for order in range(28, 0, -2):
        value = 1.0 - value * square / (order * (order - 1.0))
    return sign * value


COS = cos_table()


def cosine(index):
    return COS[np.mod(index, TS)]


def sine(index):
    return COS[np.mod(index - TS // 4, TS)]


def split(table):
    high = np.asarray(table, np.float32).astype(BF)
    low = (table - high.astype(np.float64)).astype(np.float32).astype(BF)
    return high, low


def bin_slots():
    bins = np.full((KN, SLOT), -1, np.int64)
    flipped = np.zeros((KN, SLOT), bool)
    for residue in range(KN):
        found = [(k, False) for k in range(F0, F0 + NF) if k % QN == residue]
        if residue:
            found += [(k, True) for k in range(F0, F0 + NF) if k % QN == QN - residue]
        for slot, (k, conj) in enumerate(found):
            bins[residue, slot] = k
            flipped[residue, slot] = conj
    return bins, flipped


def first_matrix():
    residue = np.arange(KN)[:, None]
    q = np.arange(QN)[None, :]
    weights = np.zeros((2 * KPAD, QPAD))
    weights[:KN, :QN] = cosine(PN * residue * q)
    weights[KPAD : KPAD + KN, :QN] = -sine(PN * residue * q)
    high, low = split(weights)
    zero = np.zeros_like(low)
    return np.concatenate(
        [np.concatenate([high, high], 1), np.concatenate([low, zero], 1)], 0
    )


def second_matrix():
    bins, flipped = bin_slots()
    p = np.arange(PN)
    weights = np.zeros((KN, GROUP, 2 * PN))
    cos = cosine(bins[:, :, None] * p)
    sin = sine(bins[:, :, None] * p)
    sign = np.where(flipped, -1.0, 1.0)[:, :, None]
    live = (bins >= 0).astype(np.float64)[:, :, None]
    weights[:, :SLOT, :PN] = live * cos
    weights[:, :SLOT, PN:] = live * sign * sin
    weights[:, SLOT:, :PN] = -live * sin
    weights[:, SLOT:, PN:] = live * sign * cos
    high, low = split(weights)
    return np.concatenate([high, low], 1)


def basis(table):
    rest = table.copy()
    columns = []
    for _ in range(HALF):
        norms = (rest * rest).sum(0)
        column = rest[:, int(norms.argmax())]
        for _ in range(2):
            for other in columns:
                column = column - other * np.cumsum(other * column)[-1]
        column = column / np.sqrt(np.cumsum(column * column)[-1])
        columns.append(column)
        rest = rest - column[:, None] * (column[:, None] * rest).sum(0)[None]
    return columns


@functools.lru_cache(None)
def lag_factors():
    bins, _ = bin_slots()
    live = (bins >= 0).astype(np.float64)
    lag = np.arange(MAXLAG + 1)[:, None]
    band = np.arange(F0, F0 + NF)[None, :]
    even_table = cosine(lag * band)
    odd_table = sine(lag[1:] * band)
    even = basis(even_table)
    odd = basis(odd_table)
    inner = np.zeros((RANK, KN, 2, SLOT))
    place = np.maximum(bins - F0, 0)
    for i in range(HALF):
        row = (even[i][:, None] * even_table).sum(0)[place] * live
        inner[i, :, 0] = row
        inner[i, :, 1] = row
        row = (odd[i][:, None] * odd_table).sum(0)[place] * live
        inner[HALF + i, :, 0] = -row
        inner[HALF + i, :, 1] = row
    outer = np.zeros((LAGS, RANK))
    for i in range(HALF):
        outer[MAXLAG:, i] = even[i]
        outer[MAXLAG::-1, i] = even[i]
        outer[MAXLAG + 1 :, HALF + i] = -odd[i]
        outer[MAXLAG - 1 :: -1, HALF + i] = odd[i]
    return outer, inner.reshape(RANK, FN).astype(np.float32)


def halves(value):
    high = value.astype(BF)
    low = (value - high.astype(F32)).astype(BF)
    return high, low


def dot(left, right):
    return jnp.dot(left, right, preferred_element_type=F32)


def spectrum_kernel(
    pairs_ref, count_ref, x_hbm, first_hbm, second_hbm, out_ref,
    xs, first, second, pad, ts, zs, ss, sems,
):
    def load(g):
        return pltpu.make_async_copy(
            x_hbm.at[:, pl.ds(g * STEP, STEP), :], xs.at[g], sems.at[g]
        )

    first_copy = pltpu.make_async_copy(first_hbm, first, sems.at[STEPS])
    second_copy = pltpu.make_async_copy(second_hbm, second, sems.at[STEPS + 1])
    first_copy.start()
    for g in range(STEPS):
        load(g).start()
    second_copy.start()
    pad[72:80, :] = jnp.zeros((8, STEP * 128), F32)

    def sections(g, carry):
        load(g).wait()
        flat = xs.at[g].reshape(QN * STEP, 128)
        for s in range(STEP):
            pad[0:QN, s * 128 : (s + 1) * 128] = flat[pl.ds(s, QN, stride=STEP), :]
        for pair in range(STEP // 2):
            high, low = halves(pad[:, pair * 256 : (pair + 1) * 256])
            both = dot(first[...], jnp.concatenate([high, low], 0))
            section = both[: 2 * KPAD] + both[2 * KPAD :]
            for side in range(2):
                p = g * STEP + pair * 2 + side
                part = section[:, side * 128 : (side + 1) * 128]
                ts[pl.ds(p, KPAD, stride=2 * PN), :] = part[:KPAD]
                ts[pl.ds(PN + p, KPAD, stride=2 * PN), :] = part[KPAD:]
        return carry

    first_copy.wait()
    lax.fori_loop(0, STEPS, sections, 0)
    second_copy.wait()

    def residue(k, power):
        high, low = halves(ts[pl.ds(pl.multiple_of(k * 2 * PN, 2 * PN), 2 * PN), :])
        product = dot(second[k], jnp.concatenate([high, low], 1))
        value = product[:GROUP, :128] + (product[:GROUP, 128:] + product[GROUP:, :128])
        zs[pl.ds(pl.multiple_of(k * GROUP, GROUP), GROUP), :] = value
        return power + jnp.sum((value * value).reshape(GROUP // 8, 8, 128), axis=0)

    power = lax.fori_loop(0, KN, residue, jnp.zeros((8, 128), F32), unroll=UNROLL)
    power = jnp.sum(power, axis=0, keepdims=True)
    factor = lax.rsqrt(power * (1.0 / NF) + EPSILON)
    out_ref[0:FN, :] = (zs[...] * factor).astype(BF)
    lane = lax.broadcasted_iota(jnp.int32, (8, 128), 1)
    sub = lax.broadcasted_iota(jnp.int32, (8, 128), 0)
    pick = jnp.where(lane == sub * (128 // VS), 1.0, 0.0).astype(BF)
    rows = lax.dot_general(
        pick, out_ref[0:FN, :], (((1,), (1,)), ((), ())), preferred_element_type=F32
    )
    ss[...] = jnp.zeros_like(ss)
    for j in range(VS):
        for c in range(CHUNKS):
            ss[j * SRC + c : j * SRC + c + 1, :] = rows[j : j + 1, c * 128 : (c + 1) * 128]
    owner = lax.axis_index("fibre")
    lane = lax.broadcasted_iota(jnp.int32, (1, 128), 1)
    table = jnp.where(lane == 2 * MAXP, count_ref[0], 0)
    for slot in range(MAXP):
        for side in range(2):
            offset = pairs_ref[side, slot] - owner
            table = jnp.where(lane == slot * 2 + side, offset, table)
    ss[TABLE - FN : TABLE - FN + 1, :] = table.astype(F32)
    out_ref[FN:ROWS, :] = ss[...].astype(BF)


def in_hbm(array):
    return pltpu.with_memory_space_constraint(array, pltpu.HBM)


def spectra(pair_blocks, pair_count, samples):
    smem = pl.BlockSpec(memory_space=pltpu.SMEM)
    vmem = pl.BlockSpec(memory_space=pltpu.VMEM)
    hbm = pl.BlockSpec(memory_space=pltpu.HBM)
    first = jnp.asarray(first_matrix())
    second = jnp.asarray(second_matrix())
    return pl.pallas_call(
        spectrum_kernel,
        in_specs=[smem, smem, hbm, hbm, hbm],
        out_specs=vmem,
        out_shape=jax.ShapeDtypeStruct((ROWS, 128), BF),
        scratch_shapes=[
            pltpu.VMEM((STEPS, QN, STEP, 128), F32),
            pltpu.VMEM(first.shape, BF),
            pltpu.VMEM(second.shape, BF),
            pltpu.VMEM((QPAD, STEP * 128), F32),
            pltpu.VMEM((KPAD * 2 * PN, 128), F32),
            pltpu.VMEM((FN, 128), F32),
            pltpu.VMEM((TAIL, 128), F32),
            pltpu.SemaphoreType.DMA((STEPS + 2,)),
        ],
        compiler_params=pltpu.CompilerParams(vmem_limit_bytes=FRONT_VMEM),
        name="spectra",
    )(
        in_hbm(pair_blocks), pair_count, in_hbm(samples), in_hbm(first), in_hbm(second)
    )


def pairs_kernel(b0, b1, b2, b3, b4, inner_ref, out_ref, receiver, source, weights):
    blocks = (b0, b1, b2, b3, b4)
    even = lax.rem(lax.axis_index("fibre"), 2) == 0
    tail = jnp.where(even, b4[FN:ROWS, :].astype(F32), b0[FN:ROWS, :].astype(F32))
    row = tail[TABLE - FN : TABLE - FN + 1, :].astype(jnp.int32)
    lane = lax.broadcasted_iota(jnp.int32, (1, 128), 1)

    def entry(index):
        return jnp.sum(jnp.where(lane == index, row, 0))

    def place_of(offset):
        return jnp.where(even, REACH - offset, offset)

    count = entry(2 * MAXP)
    spot = lax.broadcasted_iota(jnp.int32, (TAIL, 128), 1)
    real_spot = lax.rem(spot, GROUP) < SLOT

    def one_pair(slot, carry):
        first = place_of(entry(2 * slot))
        second = place_of(entry(2 * slot + 1))
        for place, block in enumerate(blocks):

            @pl.when(second == place)
            def _():
                receiver[...] = block[0:FN, :]

            @pl.when(first == place)
            def _():
                source[...] = block[FN:ROWS, :].astype(F32)

        straight = source[...]
        crossed = jnp.where(
            real_spot, pltpu.roll(straight, 128 - SLOT, 1), pltpu.roll(straight, SLOT, 1)
        )
        for j in range(VS):
            for c in range(CHUNKS):
                at = j * SRC + c
                here = pl.ds(c * 128, 128)
                even = inner_ref[0:HALF, here] * straight[at : at + 1, :]
                odd = inner_ref[HALF:RANK, here] * crossed[at : at + 1, :]
                weights[j * RANK : j * RANK + HALF, here] = even.astype(BF)
                weights[j * RANK + HALF : (j + 1) * RANK, here] = odd.astype(BF)
        result = dot(weights[...], receiver[...]).astype(BF)
        for j in range(VS):
            out_ref[slot * VS + j] = result[j * RANK : (j + 1) * RANK]
        return carry

    def one_blank(slot, carry):
        for j in range(VS):
            out_ref[slot * VS + j] = jnp.zeros((RANK, 128), BF)
        return carry

    lax.fori_loop(0, count, one_pair, 0)
    lax.fori_loop(count, MAXP, one_blank, 0)


def pair_rows(blocks):
    _, inner = lag_factors()
    vmem = pl.BlockSpec(memory_space=pltpu.VMEM)
    return pl.pallas_call(
        pairs_kernel,
        in_specs=[vmem] * 6,
        out_specs=vmem,
        out_shape=jax.ShapeDtypeStruct((MAXP * VS, RANK, 128), BF),
        scratch_shapes=[
            pltpu.VMEM((FN, 128), BF),
            pltpu.VMEM((TAIL, 128), F32),
            pltpu.VMEM((VS * RANK, FN), BF),
        ],
        compiler_params=pltpu.CompilerParams(vmem_limit_bytes=28 * 2**20),
        name="pair_rows",
    )(*blocks, jnp.asarray(inner))


def lags_kernel(row_ref, outer_ref, out_ref):
    row = row_ref[...]
    out_ref[:, 0, :] = dot(outer_ref[...], jnp.concatenate([row, row], 0))


def lag_rows(row):
    outer, _ = lag_factors()
    high, low = split(outer)
    table = jnp.asarray(np.concatenate([high, low], 1))
    vmem = pl.BlockSpec(memory_space=pltpu.VMEM)
    return pl.pallas_call(
        lags_kernel,
        in_specs=[vmem, vmem],
        out_specs=vmem,
        out_shape=jax.ShapeDtypeStruct((LAGS, 1, 128), F32),
        compiler_params=pltpu.CompilerParams(vmem_limit_bytes=8 * 2**20),
        name="lag_rows",
    )(row, table)


def turned(array, by):
    size = lax.axis_size("fibre")
    return lax.ppermute(array, "fibre", [(i, (i + by) % size) for i in range(size)])


def swapped(array):
    size = lax.axis_size("fibre")
    return lax.ppermute(array, "fibre", [(i, i ^ 1) for i in range(size)])


def parted(array, by):
    size = lax.axis_size("fibre")
    return lax.ppermute(
        array, "fibre", [(i, (i - by if i % 2 == 0 else i + by) % size) for i in range(size)]
    )


def gathered(own):
    early = parted(own, 2)
    late = parted(own, -2)
    sibling = swapped(own)
    other = swapped(early)
    return [early, sibling, own, other, late]


def shards(recordings, pair_blocks, pair_count):
    samples = recordings.reshape(QN, PN, 128)
    own = spectra(pair_blocks[0].T, pair_count, samples)
    rows = pair_rows(gathered(own))
    shared = lax.all_to_all(rows, "tm", 0, 0)
    row = (jnp.sum(shared.astype(F32), axis=0) * (1.0 / math.sqrt(NF * shared.shape[0]))).astype(BF)
    return lag_rows(turned(row, -2))[None].transpose(0, 2, 1, 3)


def solution(mesh):
    in_specs = (P("tm", "fibre", None, None), P("fibre", None, None), P("fibre"))
    out_specs = P("fibre", "tm", None, None)
    return jax.shard_map(shards, mesh=mesh, in_specs=in_specs, out_specs=out_specs, check_vma=False)
```

```python
import functools
import math

import jax
import jax.numpy as jnp
import numpy as np
from jax import lax
from jax.experimental import pallas as pl
from jax.experimental.pallas import tpu as pltpu
from jax.sharding import PartitionSpec as P

TS = 6000
F0 = 60
NF = 1152
MAXLAG = 200
LAGS = 401
VS = 2
REACH = 4
MAXP = 4
EPSILON = 1e-06

QN = 75
PN = 80
KN = 38
KPAD = 40
QPAD = 80
WIDE = 2 * PN + 8
SLOT = 32
GROUP = 2 * SLOT
FN = KN * GROUP
CHUNKS = FN // 128
SRC = 24
TAIL = 2 * SRC
ROWS = FN + TAIL
TABLE = FN + 2 * SRC - 1
HALF = 96
RANK = 2 * HALF
STEP = 40
STEPS = PN // STEP
UNROLL = 19
FRONT_VMEM = 28 * 2**20
BF = jnp.bfloat16
F32 = jnp.float32


def cos_table():
    index = np.arange(TS)
    folded = np.minimum(index, TS - index)
    sign = np.where(folded > TS // 4, -1.0, 1.0)
    folded = np.where(folded > TS // 4, TS // 2 - folded, folded)
    square = (folded * (2.0 * math.pi / TS)) ** 2
    value = np.ones(TS)
    for order in range(28, 0, -2):
        value = 1.0 - value * square / (order * (order - 1.0))
    return sign * value


COS = cos_table()


def cosine(index):
    return COS[np.mod(index, TS)]


def sine(index):
    return COS[np.mod(index - TS // 4, TS)]


def split(table):
    high = np.asarray(table, np.float32).astype(BF)
    low = (table - high.astype(np.float64)).astype(np.float32).astype(BF)
    return high, low


def bin_slots():
    bins = np.full((KN, SLOT), -1, np.int64)
    flipped = np.zeros((KN, SLOT), bool)
    for residue in range(KN):
        found = [(k, False) for k in range(F0, F0 + NF) if k % QN == residue]
        if residue:
            found += [(k, True) for k in range(F0, F0 + NF) if k % QN == QN - residue]
        for slot, (k, conj) in enumerate(found):
            bins[residue, slot] = k
            flipped[residue, slot] = conj
    return bins, flipped


def first_matrix():
    residue = np.arange(KN)[:, None]
    q = np.arange(QN)[None, :]
    weights = np.zeros((2 * KPAD, QPAD))
    weights[:KN, :QN] = cosine(PN * residue * q)
    weights[KPAD : KPAD + KN, :QN] = -sine(PN * residue * q)
    high, low = split(weights)
    zero = np.zeros_like(low)
    return np.concatenate(
        [np.concatenate([high, high], 1), np.concatenate([low, zero], 1)], 0
    )


def second_matrix():
    bins, flipped = bin_slots()
    p = np.arange(PN)
    weights = np.zeros((KN, GROUP, 2 * PN))
    cos = cosine(bins[:, :, None] * p)
    sin = sine(bins[:, :, None] * p)
    sign = np.where(flipped, -1.0, 1.0)[:, :, None]
    live = (bins >= 0).astype(np.float64)[:, :, None]
    weights[:, :SLOT, :PN] = live * cos
    weights[:, :SLOT, PN:] = live * sign * sin
    weights[:, SLOT:, :PN] = -live * sin
    weights[:, SLOT:, PN:] = live * sign * cos
    high, low = split(weights)
    return np.concatenate([high, low], 1)


def basis(table):
    rest = table.copy()
    columns = []
    for _ in range(HALF):
        norms = (rest * rest).sum(0)
        column = rest[:, int(norms.argmax())]
        for _ in range(2):
            for other in columns:
                column = column - other * np.cumsum(other * column)[-1]
        column = column / np.sqrt(np.cumsum(column * column)[-1])
        columns.append(column)
        rest = rest - column[:, None] * (column[:, None] * rest).sum(0)[None]
    return columns


@functools.lru_cache(None)
def lag_factors():
    bins, _ = bin_slots()
    live = (bins >= 0).astype(np.float64)
    lag = np.arange(MAXLAG + 1)[:, None]
    band = np.arange(F0, F0 + NF)[None, :]
    even_table = cosine(lag * band)
    odd_table = sine(lag[1:] * band)
    even = basis(even_table)
    odd = basis(odd_table)
    inner = np.zeros((RANK, KN, 2, SLOT))
    place = np.maximum(bins - F0, 0)
    for i in range(HALF):
        row = (even[i][:, None] * even_table).sum(0)[place] * live
        inner[i, :, 0] = row
        inner[i, :, 1] = row
        row = (odd[i][:, None] * odd_table).sum(0)[place] * live
        inner[HALF + i, :, 0] = -row
        inner[HALF + i, :, 1] = row
    outer = np.zeros((LAGS, RANK))
    for i in range(HALF):
        outer[MAXLAG:, i] = even[i]
        outer[MAXLAG::-1, i] = even[i]
        outer[MAXLAG + 1 :, HALF + i] = -odd[i]
        outer[MAXLAG - 1 :: -1, HALF + i] = odd[i]
    return outer, inner.reshape(RANK, FN).astype(np.float32)


def halves(value):
    high = value.astype(BF)
    low = (value - high.astype(F32)).astype(BF)
    return high, low


def dot(left, right):
    return jnp.dot(left, right, preferred_element_type=F32)


def spectrum_kernel(
    pairs_hbm, count_ref, x_hbm, first_hbm, second_hbm, out_ref,
    pairs_ref, xs, first, second, pad, ts, zs, ss, sems,
):
    def load(g):
        return pltpu.make_async_copy(
            x_hbm.at[:, pl.ds(g * STEP, STEP), :], xs.at[g], sems.at[g]
        )

    first_copy = pltpu.make_async_copy(first_hbm, first, sems.at[STEPS])
    second_copy = pltpu.make_async_copy(second_hbm, second, sems.at[STEPS + 1])
    first_copy.start()
    for g in range(STEPS):
        load(g).start()
    second_copy.start()
    pairs_copy = pltpu.make_async_copy(pairs_hbm, pairs_ref, sems.at[STEPS + 2])
    pairs_copy.start()
    pad[72:80, :] = jnp.zeros((8, STEP * 128), F32)

    def sections(g, carry):
        load(g).wait()
        flat = xs.at[g].reshape(QN * STEP, 128)
        for s in range(STEP):
            pad[0:QN, s * 128 : (s + 1) * 128] = flat[pl.ds(s, QN, stride=STEP), :]
        for pair in range(STEP // 2):
            high, low = halves(pad[:, pair * 256 : (pair + 1) * 256])
            both = dot(first[...], jnp.concatenate([high, low], 0))
            section = both[: 2 * KPAD] + both[2 * KPAD :]
            for side in range(2):
                p = g * STEP + pair * 2 + side
                part = section[:, side * 128 : (side + 1) * 128]
                ts[pl.ds(p, KPAD, stride=WIDE), :] = part[:KPAD]
                ts[pl.ds(PN + p, KPAD, stride=WIDE), :] = part[KPAD:]
        return carry

    first_copy.wait()
    lax.fori_loop(0, STEPS, sections, 0)
    second_copy.wait()

    def residue(k, power):
        high, low = halves(ts[pl.ds(pl.multiple_of(k * WIDE, 8), 2 * PN), :])
        product = dot(second[k], jnp.concatenate([high, low], 1))
        value = product[:GROUP, :128] + (product[:GROUP, 128:] + product[GROUP:, :128])
        zs[pl.ds(pl.multiple_of(k * GROUP, GROUP), GROUP), :] = value
        return power + jnp.sum((value * value).reshape(GROUP // 8, 8, 128), axis=0)

    power = lax.fori_loop(0, KN, residue, jnp.zeros((8, 128), F32), unroll=UNROLL)
    power = jnp.sum(power, axis=0, keepdims=True)
    factor = lax.rsqrt(power * (1.0 / NF) + EPSILON)
    out_ref[0:FN, :] = (zs[...] * factor).astype(BF)
    lane = lax.broadcasted_iota(jnp.int32, (8, 128), 1)
    sub = lax.broadcasted_iota(jnp.int32, (8, 128), 0)
    pick = jnp.where(lane == sub * (128 // VS), 1.0, 0.0).astype(BF)
    rows = lax.dot_general(
        pick, out_ref[0:FN, :], (((1,), (1,)), ((), ())), preferred_element_type=F32
    )
    ss[...] = jnp.zeros_like(ss)
    for j in range(VS):
        for c in range(CHUNKS):
            ss[j * SRC + c : j * SRC + c + 1, :] = rows[j : j + 1, c * 128 : (c + 1) * 128]
    pairs_copy.wait()
    owner = lax.axis_index("fibre")
    lane = lax.broadcasted_iota(jnp.int32, (1, 128), 1)
    table = jnp.where(lane == 2 * MAXP, count_ref[0], 0)
    for slot in range(MAXP):
        for side in range(2):
            offset = pairs_ref[side, slot] - owner
            table = jnp.where(lane == slot * 2 + side, offset, table)
    ss[TABLE - FN : TABLE - FN + 1, :] = table.astype(F32)
    out_ref[FN:ROWS, :] = ss[...].astype(BF)


def in_hbm(array):
    return pltpu.with_memory_space_constraint(array, pltpu.HBM)


def spectra(pair_blocks, pair_count, samples):
    vmem = pl.BlockSpec(memory_space=pltpu.VMEM)
    hbm = pl.BlockSpec(memory_space=pltpu.HBM)
    first = jnp.asarray(first_matrix())
    second = jnp.asarray(second_matrix())
    return pl.pallas_call(
        spectrum_kernel,
        in_specs=[hbm, pl.BlockSpec(memory_space=pltpu.SMEM), hbm, hbm, hbm],
        out_specs=vmem,
        out_shape=jax.ShapeDtypeStruct((ROWS, 128), BF),
        scratch_shapes=[
            pltpu.SMEM(pair_blocks.shape, jnp.int32),
            pltpu.VMEM((STEPS, QN, STEP, 128), F32),
            pltpu.VMEM(first.shape, BF),
            pltpu.VMEM(second.shape, BF),
            pltpu.VMEM((QPAD, STEP * 128), F32),
            pltpu.VMEM((KPAD * WIDE, 128), F32),
            pltpu.VMEM((FN, 128), F32),
            pltpu.VMEM((TAIL, 128), F32),
            pltpu.SemaphoreType.DMA((STEPS + 3,)),
        ],
        compiler_params=pltpu.CompilerParams(vmem_limit_bytes=FRONT_VMEM),
        name="spectra",
    )(
        in_hbm(pair_blocks), pair_count, in_hbm(samples), in_hbm(first), in_hbm(second)
    )


def pairs_kernel(b0, b1, b2, b3, b4, inner_ref, out_ref, receiver, source, weights):
    blocks = (b0, b1, b2, b3, b4)
    even = lax.rem(lax.axis_index("fibre"), 2) == 0
    tail = jnp.where(even, b4[FN:ROWS, :].astype(F32), b0[FN:ROWS, :].astype(F32))
    row = tail[TABLE - FN : TABLE - FN + 1, :].astype(jnp.int32)
    lane = lax.broadcasted_iota(jnp.int32, (1, 128), 1)

    def entry(index):
        return jnp.sum(jnp.where(lane == index, row, 0))

    def place_of(offset):
        return jnp.where(even, REACH - offset, offset)

    count = entry(2 * MAXP)
    spot = lax.broadcasted_iota(jnp.int32, (TAIL, 128), 1)
    real_spot = lax.rem(spot, GROUP) < SLOT

    def one_pair(slot, carry):
        first = place_of(entry(2 * slot))
        second = place_of(entry(2 * slot + 1))
        for place, block in enumerate(blocks):

            @pl.when(second == place)
            def _():
                receiver[...] = block[0:FN, :]

            @pl.when(first == place)
            def _():
                source[...] = block[FN:ROWS, :].astype(F32)

        straight = source[...]
        crossed = jnp.where(
            real_spot, pltpu.roll(straight, 128 - SLOT, 1), pltpu.roll(straight, SLOT, 1)
        )
        for j in range(VS):
            for c in range(CHUNKS):
                at = j * SRC + c
                here = pl.ds(c * 128, 128)
                even = inner_ref[0:HALF, here] * straight[at : at + 1, :]
                odd = inner_ref[HALF:RANK, here] * crossed[at : at + 1, :]
                weights[j * RANK : j * RANK + HALF, here] = even.astype(BF)
                weights[j * RANK + HALF : (j + 1) * RANK, here] = odd.astype(BF)
        result = dot(weights[...], receiver[...]).astype(BF)
        for j in range(VS):
            out_ref[slot * VS + j] = result[j * RANK : (j + 1) * RANK]
        return carry

    def one_blank(slot, carry):
        for j in range(VS):
            out_ref[slot * VS + j] = jnp.zeros((RANK, 128), BF)
        return carry

    lax.fori_loop(0, count, one_pair, 0)
    lax.fori_loop(count, MAXP, one_blank, 0)


def pair_rows(blocks):
    _, inner = lag_factors()
    vmem = pl.BlockSpec(memory_space=pltpu.VMEM)
    return pl.pallas_call(
        pairs_kernel,
        in_specs=[vmem] * 6,
        out_specs=vmem,
        out_shape=jax.ShapeDtypeStruct((MAXP * VS, RANK, 128), BF),
        scratch_shapes=[
            pltpu.VMEM((FN, 128), BF),
            pltpu.VMEM((TAIL, 128), F32),
            pltpu.VMEM((VS * RANK, FN), BF),
        ],
        compiler_params=pltpu.CompilerParams(vmem_limit_bytes=28 * 2**20),
        name="pair_rows",
    )(*blocks, jnp.asarray(inner))


def lags_kernel(row_ref, outer_ref, out_ref):
    row = row_ref[...]
    out_ref[:, 0, :] = dot(outer_ref[...], jnp.concatenate([row, row], 0))


def lag_rows(row):
    outer, _ = lag_factors()
    high, low = split(outer)
    table = jnp.asarray(np.concatenate([high, low], 1))
    vmem = pl.BlockSpec(memory_space=pltpu.VMEM)
    return pl.pallas_call(
        lags_kernel,
        in_specs=[vmem, vmem],
        out_specs=vmem,
        out_shape=jax.ShapeDtypeStruct((LAGS, 1, 128), F32),
        compiler_params=pltpu.CompilerParams(vmem_limit_bytes=8 * 2**20),
        name="lag_rows",
    )(row, table)


def turned(array, by):
    size = lax.axis_size("fibre")
    return lax.ppermute(array, "fibre", [(i, (i + by) % size) for i in range(size)])


def swapped(array):
    size = lax.axis_size("fibre")
    return lax.ppermute(array, "fibre", [(i, i ^ 1) for i in range(size)])


def parted(array, by):
    size = lax.axis_size("fibre")
    return lax.ppermute(
        array, "fibre", [(i, (i - by if i % 2 == 0 else i + by) % size) for i in range(size)]
    )


def gathered(own):
    early = parted(own, 2)
    late = parted(own, -2)
    sibling = swapped(own)
    other = swapped(early)
    return [early, sibling, own, other, late]


def shards(recordings, pair_blocks, pair_count):
    samples = recordings.reshape(QN, PN, 128)
    own = spectra(pair_blocks[0].T, pair_count, samples)
    rows = pair_rows(gathered(own))
    shared = lax.all_to_all(rows, "tm", 0, 0)
    row = (jnp.sum(shared.astype(F32), axis=0) * (1.0 / math.sqrt(NF * shared.shape[0]))).astype(BF)
    return lag_rows(turned(row, -2))[None].transpose(0, 2, 1, 3)


def solution(mesh):
    in_specs = (P("tm", "fibre", None, None), P("fibre", None, None), P("fibre"))
    out_specs = P("fibre", "tm", None, None)
    return jax.shard_map(shards, mesh=mesh, in_specs=in_specs, out_specs=out_specs, check_vma=False)
```

```python
import functools
import math

import jax
import jax.numpy as jnp
import numpy as np
from jax import lax
from jax.experimental import pallas as pl
from jax.experimental.pallas import tpu as pltpu
from jax.sharding import PartitionSpec as P

TS = 6000
F0 = 60
NF = 1152
MAXLAG = 200
LAGS = 401
VS = 2
REACH = 4
MAXP = 4
EPSILON = 1e-06

QN = 75
PN = 80
KN = 38
KPAD = 40
QPAD = 80
WIDE = 2 * PN + 8
SLOT = 32
GROUP = 2 * SLOT
FN = KN * GROUP
BINS = KN * SLOT
CHUNKS = -(-BINS // 128)
TAIL = 48
ROWS = FN + TAIL
TABLE = ROWS - 1
HALF = 96
RANK = 2 * HALF
STEP = 40
STEPS = PN // STEP
UNROLL = 19
FRONT_VMEM = 28 * 2**20
BF = jnp.bfloat16
F32 = jnp.float32


def cos_table():
    index = np.arange(TS)
    folded = np.minimum(index, TS - index)
    sign = np.where(folded > TS // 4, -1.0, 1.0)
    folded = np.where(folded > TS // 4, TS // 2 - folded, folded)
    square = (folded * (2.0 * math.pi / TS)) ** 2
    value = np.ones(TS)
    for order in range(28, 0, -2):
        value = 1.0 - value * square / (order * (order - 1.0))
    return sign * value


COS = cos_table()


def cosine(index):
    return COS[np.mod(index, TS)]


def sine(index):
    return COS[np.mod(index - TS // 4, TS)]


def split(table):
    high = np.asarray(table, np.float32).astype(BF)
    low = (table - high.astype(np.float64)).astype(np.float32).astype(BF)
    return high, low


def bin_slots():
    bins = np.full((KN, SLOT), -1, np.int64)
    flipped = np.zeros((KN, SLOT), bool)
    for residue in range(KN):
        found = [(k, False) for k in range(F0, F0 + NF) if k % QN == residue]
        if residue:
            found += [(k, True) for k in range(F0, F0 + NF) if k % QN == QN - residue]
        for slot, (k, conj) in enumerate(found):
            bins[residue, slot] = k
            flipped[residue, slot] = conj
    return bins, flipped


def first_matrix():
    residue = np.arange(KN)[:, None]
    q = np.arange(QN)[None, :]
    weights = np.zeros((2 * KPAD, QPAD))
    weights[:KN, :QN] = cosine(PN * residue * q)
    weights[KPAD : KPAD + KN, :QN] = -sine(PN * residue * q)
    high, low = split(weights)
    zero = np.zeros_like(low)
    return np.concatenate(
        [np.concatenate([high, high], 1), np.concatenate([low, zero], 1)], 0
    )


def second_matrix():
    bins, flipped = bin_slots()
    p = np.arange(PN)
    weights = np.zeros((KN, GROUP, 2 * PN))
    cos = cosine(bins[:, :, None] * p)
    sin = sine(bins[:, :, None] * p)
    sign = np.where(flipped, -1.0, 1.0)[:, :, None]
    live = (bins >= 0).astype(np.float64)[:, :, None]
    weights[:, :SLOT, :PN] = live * cos
    weights[:, :SLOT, PN:] = live * sign * sin
    weights[:, SLOT:, :PN] = -live * sin
    weights[:, SLOT:, PN:] = live * sign * cos
    high, low = split(weights)
    return np.concatenate([high, low], 1)


def basis(table):
    rest = table.copy()
    columns = []
    for _ in range(HALF):
        norms = (rest * rest).sum(0)
        column = rest[:, int(norms.argmax())]
        for _ in range(2):
            for other in columns:
                column = column - other * np.cumsum(other * column)[-1]
        column = column / np.sqrt(np.cumsum(column * column)[-1])
        columns.append(column)
        rest = rest - column[:, None] * (column[:, None] * rest).sum(0)[None]
    return columns


@functools.lru_cache(None)
def lag_factors():
    bins, _ = bin_slots()
    live = (bins >= 0).astype(np.float64)
    lag = np.arange(MAXLAG + 1)[:, None]
    band = np.arange(F0, F0 + NF)[None, :]
    even_table = cosine(lag * band)
    odd_table = sine(lag[1:] * band)
    even = basis(even_table)
    odd = basis(odd_table)
    inner = np.zeros((2, HALF, KN, SLOT))
    place = np.maximum(bins - F0, 0)
    for i in range(HALF):
        inner[0, i] = (even[i][:, None] * even_table).sum(0)[place] * live
        inner[1, i] = (odd[i][:, None] * odd_table).sum(0)[place] * live
    outer = np.zeros((LAGS, RANK))
    for i in range(HALF):
        outer[MAXLAG:, i] = even[i]
        outer[MAXLAG::-1, i] = even[i]
        outer[MAXLAG + 1 :, HALF + i] = -odd[i]
        outer[MAXLAG - 1 :: -1, HALF + i] = odd[i]
    return outer, inner.reshape(RANK, BINS).astype(np.float32)


def halves(value):
    high = value.astype(BF)
    low = (value - high.astype(F32)).astype(BF)
    return high, low


def dot(left, right):
    return jnp.dot(left, right, preferred_element_type=F32)


def spectrum_kernel(
    pairs_hbm, count_ref, x_hbm, first_hbm, second_hbm, out_ref,
    pairs_ref, xs, first, second, pad, ts, zs, ss, sems,
):
    def load(g):
        return pltpu.make_async_copy(
            x_hbm.at[:, pl.ds(g * STEP, STEP), :], xs.at[g], sems.at[g]
        )

    first_copy = pltpu.make_async_copy(first_hbm, first, sems.at[STEPS])
    second_copy = pltpu.make_async_copy(second_hbm, second, sems.at[STEPS + 1])
    first_copy.start()
    for g in range(STEPS):
        load(g).start()
    second_copy.start()
    pairs_copy = pltpu.make_async_copy(pairs_hbm, pairs_ref, sems.at[STEPS + 2])
    pairs_copy.start()
    pad[72:80, :] = jnp.zeros((8, STEP * 128), F32)

    def sections(g, carry):
        load(g).wait()
        flat = xs.at[g].reshape(QN * STEP, 128)
        for s in range(STEP):
            pad[0:QN, s * 128 : (s + 1) * 128] = flat[pl.ds(s, QN, stride=STEP), :]
        for pair in range(STEP // 2):
            high, low = halves(pad[:, pair * 256 : (pair + 1) * 256])
            both = dot(first[...], jnp.concatenate([high, low], 0))
            section = both[: 2 * KPAD] + both[2 * KPAD :]
            for side in range(2):
                p = g * STEP + pair * 2 + side
                part = section[:, side * 128 : (side + 1) * 128]
                ts[pl.ds(p, KPAD, stride=WIDE), :] = part[:KPAD]
                ts[pl.ds(PN + p, KPAD, stride=WIDE), :] = part[KPAD:]
        return carry

    first_copy.wait()
    lax.fori_loop(0, STEPS, sections, 0)
    second_copy.wait()

    def residue(k, power):
        high, low = halves(ts[pl.ds(pl.multiple_of(k * WIDE, 8), 2 * PN), :])
        product = dot(second[k], jnp.concatenate([high, low], 1))
        value = product[:GROUP, :128] + (product[:GROUP, 128:] + product[GROUP:, :128])
        at = pl.multiple_of(k * SLOT, SLOT)
        zs[pl.ds(at, SLOT), :] = value[:SLOT]
        zs[pl.ds(BINS + at, SLOT), :] = value[SLOT:]
        return power + jnp.sum((value * value).reshape(GROUP // 8, 8, 128), axis=0)

    power = lax.fori_loop(0, KN, residue, jnp.zeros((8, 128), F32), unroll=UNROLL)
    power = jnp.sum(power, axis=0, keepdims=True)
    factor = lax.rsqrt(power * (1.0 / NF) + EPSILON)
    out_ref[0:FN, :] = (zs[...] * factor).astype(BF)
    lane = lax.broadcasted_iota(jnp.int32, (8, 128), 1)
    sub = lax.broadcasted_iota(jnp.int32, (8, 128), 0)
    pick = jnp.where(lane == sub * (128 // VS), 1.0, 0.0).astype(BF)
    ss[...] = jnp.zeros_like(ss)
    for part in range(2):
        rows = lax.dot_general(
            pick,
            out_ref[part * BINS : (part + 1) * BINS, :],
            (((1,), (1,)), ((), ())),
            preferred_element_type=F32,
        )
        for j in range(VS):
            for c in range(CHUNKS):
                at = (j * 2 + part) * CHUNKS + c
                wide = min(128, BINS - c * 128)
                ss[at : at + 1, 0:wide] = rows[j : j + 1, c * 128 : c * 128 + wide]
    pairs_copy.wait()
    owner = lax.axis_index("fibre")
    lane = lax.broadcasted_iota(jnp.int32, (1, 128), 1)
    table = jnp.where(lane == 2 * MAXP, count_ref[0], 0)
    for slot in range(MAXP):
        for side in range(2):
            offset = pairs_ref[side, slot] - owner
            table = jnp.where(lane == slot * 2 + side, offset, table)
    ss[TABLE - FN : TABLE - FN + 1, :] = table.astype(F32)
    out_ref[FN:ROWS, :] = ss[...].astype(BF)


def in_hbm(array):
    return pltpu.with_memory_space_constraint(array, pltpu.HBM)


def spectra(pair_blocks, pair_count, samples):
    vmem = pl.BlockSpec(memory_space=pltpu.VMEM)
    hbm = pl.BlockSpec(memory_space=pltpu.HBM)
    first = jnp.asarray(first_matrix())
    second = jnp.asarray(second_matrix())
    return pl.pallas_call(
        spectrum_kernel,
        in_specs=[hbm, pl.BlockSpec(memory_space=pltpu.SMEM), hbm, hbm, hbm],
        out_specs=vmem,
        out_shape=jax.ShapeDtypeStruct((ROWS, 128), BF),
        scratch_shapes=[
            pltpu.SMEM(pair_blocks.shape, jnp.int32),
            pltpu.VMEM((STEPS, QN, STEP, 128), F32),
            pltpu.VMEM(first.shape, BF),
            pltpu.VMEM(second.shape, BF),
            pltpu.VMEM((QPAD, STEP * 128), F32),
            pltpu.VMEM((KPAD * WIDE, 128), F32),
            pltpu.VMEM((FN, 128), F32),
            pltpu.VMEM((TAIL, 128), F32),
            pltpu.SemaphoreType.DMA((STEPS + 3,)),
        ],
        compiler_params=pltpu.CompilerParams(vmem_limit_bytes=FRONT_VMEM),
        name="spectra",
    )(
        in_hbm(pair_blocks), pair_count, in_hbm(samples), in_hbm(first), in_hbm(second)
    )


def pairs_kernel(
    b0, b1, b2, b3, b4, inner_ref, out_ref, entries, receiver, source, weights
):
    blocks = (b0, b1, b2, b3, b4)
    even = lax.rem(lax.axis_index("fibre"), 2) == 0
    tail = jnp.where(even, b4[FN:ROWS, :].astype(F32), b0[FN:ROWS, :].astype(F32))
    row = tail[TABLE - FN : TABLE - FN + 1, :].astype(jnp.int32)
    lane = lax.broadcasted_iota(jnp.int32, (1, 128), 1)
    for index in range(2 * MAXP + 1):
        entries[index] = jnp.sum(jnp.where(lane == index, row, 0))

    def place_of(offset):
        return jnp.where(even, REACH - offset, offset)

    count = entries[2 * MAXP]

    def one_pair(slot, carry):
        first = place_of(entries[2 * slot])
        second = place_of(entries[2 * slot + 1])
        for place, block in enumerate(blocks):

            @pl.when(second == place)
            def _():
                receiver[:, 0:128] = block[0:BINS, :]
                receiver[:, 128:256] = block[BINS:FN, :]

            @pl.when(first == place)
            def _():
                source[...] = block[FN:ROWS, :].astype(F32)

        for c in range(CHUNKS):
            wide = min(128, BINS - c * 128)
            here = slice(c * 128, c * 128 + wide)
            table = inner_ref[:, here]
            for part in range(2 * VS):
                at = part * CHUNKS + c
                scaled = table * source[at : at + 1, 0:wide]
                weights[part * RANK : (part + 1) * RANK, here] = scaled.astype(BF)
        product = dot(weights[...], receiver[...])
        for j in range(VS):
            real = product[(2 * j) * RANK : (2 * j + 1) * RANK]
            imag = product[(2 * j + 1) * RANK : (2 * j + 2) * RANK]
            same = real[:HALF, :128] + imag[:HALF, 128:]
            turn = real[HALF:, 128:] - imag[HALF:, :128]
            out_ref[slot * VS + j, 0:HALF, :] = same.astype(BF)
            out_ref[slot * VS + j, HALF:RANK, :] = turn.astype(BF)
        return carry

    def one_blank(slot, carry):
        for j in range(VS):
            out_ref[slot * VS + j] = jnp.zeros((RANK, 128), BF)
        return carry

    lax.fori_loop(0, count, one_pair, 0)
    lax.fori_loop(count, MAXP, one_blank, 0)


def pair_rows(blocks):
    _, inner = lag_factors()
    vmem = pl.BlockSpec(memory_space=pltpu.VMEM)
    return pl.pallas_call(
        pairs_kernel,
        in_specs=[vmem] * 6,
        out_specs=vmem,
        out_shape=jax.ShapeDtypeStruct((MAXP * VS, RANK, 128), BF),
        scratch_shapes=[
            pltpu.SMEM((2 * MAXP + 1,), jnp.int32),
            pltpu.VMEM((BINS, 256), BF),
            pltpu.VMEM((TAIL, 128), F32),
            pltpu.VMEM((2 * VS * RANK, BINS), BF),
        ],
        compiler_params=pltpu.CompilerParams(vmem_limit_bytes=28 * 2**20),
        name="pair_rows",
    )(*blocks, jnp.asarray(inner))


def lags_kernel(row_ref, outer_ref, out_ref):
    row = row_ref[...]
    out_ref[:, 0, :] = dot(outer_ref[...], jnp.concatenate([row, row], 0))


def lag_rows(row):
    outer, _ = lag_factors()
    high, low = split(outer)
    table = jnp.asarray(np.concatenate([high, low], 1))
    vmem = pl.BlockSpec(memory_space=pltpu.VMEM)
    return pl.pallas_call(
        lags_kernel,
        in_specs=[vmem, vmem],
        out_specs=vmem,
        out_shape=jax.ShapeDtypeStruct((LAGS, 1, 128), F32),
        compiler_params=pltpu.CompilerParams(vmem_limit_bytes=8 * 2**20),
        name="lag_rows",
    )(row, table)


def turned(array, by):
    size = lax.axis_size("fibre")
    return lax.ppermute(array, "fibre", [(i, (i + by) % size) for i in range(size)])


def swapped(array):
    size = lax.axis_size("fibre")
    return lax.ppermute(array, "fibre", [(i, i ^ 1) for i in range(size)])


def parted(array, by):
    size = lax.axis_size("fibre")
    return lax.ppermute(
        array, "fibre", [(i, (i - by if i % 2 == 0 else i + by) % size) for i in range(size)]
    )


def gathered(own):
    early = parted(own, 2)
    late = parted(own, -2)
    sibling = swapped(own)
    other = swapped(early)
    return [early, sibling, own, other, late]


def shards(recordings, pair_blocks, pair_count):
    samples = recordings.reshape(QN, PN, 128)
    own = spectra(pair_blocks[0].T, pair_count, samples)
    rows = pair_rows(gathered(own))
    shared = lax.all_to_all(rows, "tm", 0, 0)
    row = (jnp.sum(shared.astype(F32), axis=0) * (1.0 / math.sqrt(NF * shared.shape[0]))).astype(BF)
    return lag_rows(turned(row, -2))[None].transpose(0, 2, 1, 3)


def solution(mesh):
    in_specs = (P("tm", "fibre", None, None), P("fibre", None, None), P("fibre"))
    out_specs = P("fibre", "tm", None, None)
    return jax.shard_map(shards, mesh=mesh, in_specs=in_specs, out_specs=out_specs, check_vma=False)
```

```python
import functools
import math

import jax
import jax.numpy as jnp
import numpy as np
from jax import lax
from jax.experimental import pallas as pl
from jax.experimental.pallas import tpu as pltpu
from jax.sharding import PartitionSpec as P

TS = 6000
F0 = 60
NF = 1152
MAXLAG = 200
LAGS = 401
VS = 2
REACH = 4
MAXP = 4
EPSILON = 1e-06

QN = 75
PN = 80
KN = 38
KPAD = 40
QPAD = 80
WIDE = 2 * PN + 8
SLOT = 32
GROUP = 2 * SLOT
FN = KN * GROUP
BINS = KN * SLOT
CHUNKS = -(-BINS // 128)
TAIL = 48
ROWS = FN + TAIL
TABLE = ROWS - 1
HALF = 96
RANK = 2 * HALF
STEP = 40
STEPS = PN // STEP
UNROLL = 38
FRONT_VMEM = 28 * 2**20
BF = jnp.bfloat16
F32 = jnp.float32


def cos_table():
    index = np.arange(TS)
    folded = np.minimum(index, TS - index)
    sign = np.where(folded > TS // 4, -1.0, 1.0)
    folded = np.where(folded > TS // 4, TS // 2 - folded, folded)
    square = (folded * (2.0 * math.pi / TS)) ** 2
    value = np.ones(TS)
    for order in range(28, 0, -2):
        value = 1.0 - value * square / (order * (order - 1.0))
    return sign * value


COS = cos_table()


def cosine(index):
    return COS[np.mod(index, TS)]


def sine(index):
    return COS[np.mod(index - TS // 4, TS)]


def split(table, parts=2):
    rest = np.asarray(table, np.float64)
    found = []
    for _ in range(parts):
        found.append(rest.astype(np.float32).astype(BF))
        rest = rest - found[-1].astype(np.float64)
    return found


def bin_slots():
    bins = np.full((KN, SLOT), -1, np.int64)
    flipped = np.zeros((KN, SLOT), bool)
    for residue in range(KN):
        found = [(k, False) for k in range(F0, F0 + NF) if k % QN == residue]
        if residue:
            found += [(k, True) for k in range(F0, F0 + NF) if k % QN == QN - residue]
        for slot, (k, conj) in enumerate(found):
            bins[residue, slot] = k
            flipped[residue, slot] = conj
    return bins, flipped


def first_matrix():
    residue = np.arange(KN)[:, None]
    q = np.arange(QN)[None, :]
    weights = np.zeros((2 * KPAD, QPAD))
    weights[:KN, :QN] = cosine(PN * residue * q)
    weights[KPAD : KPAD + KN, :QN] = -sine(PN * residue * q)
    high, mid, low = split(weights, 3)
    zero = np.zeros_like(low)
    rows = ([high, high, high], [mid, mid, zero], [low, zero, zero])
    return np.concatenate([np.concatenate(row, 1) for row in rows], 0)


def second_matrix():
    bins, flipped = bin_slots()
    p = np.arange(PN)
    weights = np.zeros((KN, GROUP, 2 * PN))
    cos = cosine(bins[:, :, None] * p)
    sin = sine(bins[:, :, None] * p)
    sign = np.where(flipped, -1.0, 1.0)[:, :, None]
    live = (bins >= 0).astype(np.float64)[:, :, None]
    weights[:, :SLOT, :PN] = live * cos
    weights[:, :SLOT, PN:] = live * sign * sin
    weights[:, SLOT:, :PN] = -live * sin
    weights[:, SLOT:, PN:] = live * sign * cos
    return np.concatenate(split(weights, 3), 1)


def basis(table):
    rest = table.copy()
    columns = []
    for _ in range(HALF):
        norms = (rest * rest).sum(0)
        column = rest[:, int(norms.argmax())]
        for _ in range(2):
            for other in columns:
                column = column - other * np.cumsum(other * column)[-1]
        column = column / np.sqrt(np.cumsum(column * column)[-1])
        columns.append(column)
        rest = rest - column[:, None] * (column[:, None] * rest).sum(0)[None]
    return columns


@functools.lru_cache(None)
def lag_factors():
    bins, _ = bin_slots()
    live = (bins >= 0).astype(np.float64)
    lag = np.arange(MAXLAG + 1)[:, None]
    band = np.arange(F0, F0 + NF)[None, :]
    even_table = cosine(lag * band)
    odd_table = sine(lag[1:] * band)
    even = basis(even_table)
    odd = basis(odd_table)
    inner = np.zeros((2, HALF, KN, SLOT))
    place = np.maximum(bins - F0, 0)
    for i in range(HALF):
        inner[0, i] = (even[i][:, None] * even_table).sum(0)[place] * live
        inner[1, i] = (odd[i][:, None] * odd_table).sum(0)[place] * live
    outer = np.zeros((LAGS, RANK))
    for i in range(HALF):
        outer[MAXLAG:, i] = even[i]
        outer[MAXLAG::-1, i] = even[i]
        outer[MAXLAG + 1 :, HALF + i] = -odd[i]
        outer[MAXLAG - 1 :: -1, HALF + i] = odd[i]
    return outer, inner.reshape(RANK, BINS).astype(np.float32)


def thirds(value):
    high = value.astype(BF)
    rest = value - high.astype(F32)
    mid = rest.astype(BF)
    low = (rest - mid.astype(F32)).astype(BF)
    return high, mid, low


def dot(left, right):
    return jnp.dot(left, right, preferred_element_type=F32)


def spectrum_kernel(
    pairs_hbm, count_ref, x_hbm, first_hbm, second_hbm, out_ref,
    pairs_ref, xs, first, second, pad, ts, zs, ss, sems,
):
    def load(g):
        return pltpu.make_async_copy(
            x_hbm.at[:, pl.ds(g * STEP, STEP), :], xs.at[g], sems.at[g]
        )

    first_copy = pltpu.make_async_copy(first_hbm, first, sems.at[STEPS])
    second_copy = pltpu.make_async_copy(second_hbm, second, sems.at[STEPS + 1])
    first_copy.start()
    for g in range(STEPS):
        load(g).start()
    second_copy.start()
    pairs_copy = pltpu.make_async_copy(pairs_hbm, pairs_ref, sems.at[STEPS + 2])
    pairs_copy.start()
    pad[72:80, :] = jnp.zeros((8, STEP * 128), F32)

    def sections(g, carry):
        load(g).wait()
        flat = xs.at[g].reshape(QN * STEP, 128)
        for s in range(STEP):
            pad[0:QN, s * 128 : (s + 1) * 128] = flat[pl.ds(s, QN, stride=STEP), :]
        for pair in range(STEP // 2):
            parts = thirds(pad[:, pair * 256 : (pair + 1) * 256])
            full = dot(first[...], jnp.concatenate(parts, 0))
            section = full[: 2 * KPAD] + (full[2 * KPAD : 4 * KPAD] + full[4 * KPAD :])
            for side in range(2):
                p = g * STEP + pair * 2 + side
                part = section[:, side * 128 : (side + 1) * 128]
                ts[pl.ds(p, KPAD, stride=WIDE), :] = part[:KPAD]
                ts[pl.ds(PN + p, KPAD, stride=WIDE), :] = part[KPAD:]
        return carry

    first_copy.wait()
    lax.fori_loop(0, STEPS, sections, 0)
    second_copy.wait()

    def residue(k, power):
        high, mid, low = thirds(ts[pl.ds(pl.multiple_of(k * WIDE, 8), 2 * PN), :])
        table = second[k]
        wide = dot(table, jnp.concatenate([high, mid], 1))
        small = wide[:GROUP, 128:] + wide[GROUP : 2 * GROUP, :128]
        least = wide[GROUP : 2 * GROUP, 128:] + wide[2 * GROUP :, :128] + dot(table[:GROUP], low)
        value = wide[:GROUP, :128] + (small + least)
        at = pl.multiple_of(k * SLOT, SLOT)
        zs[pl.ds(at, SLOT), :] = value[:SLOT]
        zs[pl.ds(BINS + at, SLOT), :] = value[SLOT:]
        return power + jnp.sum((value * value).reshape(GROUP // 8, 8, 128), axis=0)

    power = lax.fori_loop(0, KN, residue, jnp.zeros((8, 128), F32), unroll=UNROLL)
    power = jnp.sum(power, axis=0, keepdims=True)
    factor = lax.rsqrt(power * (1.0 / NF) + EPSILON)
    out_ref[0:FN, :] = (zs[...] * factor).astype(BF)
    lane = lax.broadcasted_iota(jnp.int32, (8, 128), 1)
    sub = lax.broadcasted_iota(jnp.int32, (8, 128), 0)
    pick = jnp.where(lane == sub * (128 // VS), 1.0, 0.0).astype(BF)
    ss[...] = jnp.zeros_like(ss)
    for part in range(2):
        rows = lax.dot_general(
            pick,
            out_ref[part * BINS : (part + 1) * BINS, :],
            (((1,), (1,)), ((), ())),
            preferred_element_type=F32,
        )
        for j in range(VS):
            for c in range(CHUNKS):
                at = (j * 2 + part) * CHUNKS + c
                wide = min(128, BINS - c * 128)
                ss[at : at + 1, 0:wide] = rows[j : j + 1, c * 128 : c * 128 + wide]
    pairs_copy.wait()
    owner = lax.axis_index("fibre")
    lane = lax.broadcasted_iota(jnp.int32, (1, 128), 1)
    table = jnp.where(lane == 2 * MAXP, count_ref[0], 0)
    for slot in range(MAXP):
        for side in range(2):
            offset = pairs_ref[side, slot] - owner
            table = jnp.where(lane == slot * 2 + side, offset, table)
    ss[TABLE - FN : TABLE - FN + 1, :] = table.astype(F32)
    out_ref[FN:ROWS, :] = ss[...].astype(BF)


def in_hbm(array):
    return pltpu.with_memory_space_constraint(array, pltpu.HBM)


def spectra(pair_blocks, pair_count, samples):
    vmem = pl.BlockSpec(memory_space=pltpu.VMEM)
    hbm = pl.BlockSpec(memory_space=pltpu.HBM)
    first = jnp.asarray(first_matrix())
    second = jnp.asarray(second_matrix())
    return pl.pallas_call(
        spectrum_kernel,
        in_specs=[hbm, pl.BlockSpec(memory_space=pltpu.SMEM), hbm, hbm, hbm],
        out_specs=vmem,
        out_shape=jax.ShapeDtypeStruct((ROWS, 128), BF),
        scratch_shapes=[
            pltpu.SMEM(pair_blocks.shape, jnp.int32),
            pltpu.VMEM((STEPS, QN, STEP, 128), F32),
            pltpu.VMEM(first.shape, BF),
            pltpu.VMEM(second.shape, BF),
            pltpu.VMEM((QPAD, STEP * 128), F32),
            pltpu.VMEM((KPAD * WIDE, 128), F32),
            pltpu.VMEM((FN, 128), F32),
            pltpu.VMEM((TAIL, 128), F32),
            pltpu.SemaphoreType.DMA((STEPS + 3,)),
        ],
        compiler_params=pltpu.CompilerParams(vmem_limit_bytes=FRONT_VMEM),
        name="spectra",
    )(
        in_hbm(pair_blocks), pair_count, in_hbm(samples), in_hbm(first), in_hbm(second)
    )


def pairs_kernel(
    b0, b1, b2, b3, b4, inner_ref, out_ref, entries, receiver, source, weights
):
    blocks = (b0, b1, b2, b3, b4)
    even = lax.rem(lax.axis_index("fibre"), 2) == 0
    tail = jnp.where(even, b4[FN:ROWS, :].astype(F32), b0[FN:ROWS, :].astype(F32))
    row = tail[TABLE - FN : TABLE - FN + 1, :].astype(jnp.int32)
    lane = lax.broadcasted_iota(jnp.int32, (1, 128), 1)
    for index in range(2 * MAXP + 1):
        entries[index] = jnp.sum(jnp.where(lane == index, row, 0))

    def place_of(offset):
        return jnp.where(even, REACH - offset, offset)

    count = entries[2 * MAXP]

    def one_pair(slot, carry):
        first = place_of(entries[2 * slot])
        second = place_of(entries[2 * slot + 1])
        for place, block in enumerate(blocks):

            @pl.when(second == place)
            def _():
                receiver[:, 0:128] = block[0:BINS, :]
                receiver[:, 128:256] = block[BINS:FN, :]

            @pl.when(first == place)
            def _():
                source[...] = block[FN:ROWS, :].astype(F32)

        for c in range(CHUNKS):
            wide = min(128, BINS - c * 128)
            here = slice(c * 128, c * 128 + wide)
            table = inner_ref[:, here]
            for part in range(2 * VS):
                at = part * CHUNKS + c
                scaled = table * source[at : at + 1, 0:wide]
                weights[part * RANK : (part + 1) * RANK, here] = scaled.astype(BF)
        product = dot(weights[...], receiver[...])
        for j in range(VS):
            real = product[(2 * j) * RANK : (2 * j + 1) * RANK]
            imag = product[(2 * j + 1) * RANK : (2 * j + 2) * RANK]
            same = real[:HALF, :128] + imag[:HALF, 128:]
            turn = real[HALF:, 128:] - imag[HALF:, :128]
            out_ref[slot * VS + j, 0:HALF, :] = same.astype(BF)
            out_ref[slot * VS + j, HALF:RANK, :] = turn.astype(BF)
        return carry

    def one_blank(slot, carry):
        for j in range(VS):
            out_ref[slot * VS + j] = jnp.zeros((RANK, 128), BF)
        return carry

    lax.fori_loop(0, count, one_pair, 0)
    lax.fori_loop(count, MAXP, one_blank, 0)


def pair_rows(blocks):
    _, inner = lag_factors()
    vmem = pl.BlockSpec(memory_space=pltpu.VMEM)
    return pl.pallas_call(
        pairs_kernel,
        in_specs=[vmem] * 6,
        out_specs=vmem,
        out_shape=jax.ShapeDtypeStruct((MAXP * VS, RANK, 128), BF),
        scratch_shapes=[
            pltpu.SMEM((2 * MAXP + 1,), jnp.int32),
            pltpu.VMEM((BINS, 256), BF),
            pltpu.VMEM((TAIL, 128), F32),
            pltpu.VMEM((2 * VS * RANK, BINS), BF),
        ],
        compiler_params=pltpu.CompilerParams(vmem_limit_bytes=28 * 2**20),
        name="pair_rows",
    )(*blocks, jnp.asarray(inner))


def lags_kernel(row_ref, outer_ref, out_ref):
    row = row_ref[...]
    out_ref[:, 0, :] = dot(outer_ref[...], jnp.concatenate([row, row], 0))


def lag_rows(row):
    outer, _ = lag_factors()
    high, low = split(outer)
    table = jnp.asarray(np.concatenate([high, low], 1))
    vmem = pl.BlockSpec(memory_space=pltpu.VMEM)
    return pl.pallas_call(
        lags_kernel,
        in_specs=[vmem, vmem],
        out_specs=vmem,
        out_shape=jax.ShapeDtypeStruct((LAGS, 1, 128), F32),
        compiler_params=pltpu.CompilerParams(vmem_limit_bytes=8 * 2**20),
        name="lag_rows",
    )(row, table)


def turned(array, by):
    size = lax.axis_size("fibre")
    return lax.ppermute(array, "fibre", [(i, (i + by) % size) for i in range(size)])


def swapped(array):
    size = lax.axis_size("fibre")
    return lax.ppermute(array, "fibre", [(i, i ^ 1) for i in range(size)])


def parted(array, by):
    size = lax.axis_size("fibre")
    return lax.ppermute(
        array, "fibre", [(i, (i - by if i % 2 == 0 else i + by) % size) for i in range(size)]
    )


def gathered(own):
    early = parted(own, 2)
    late = parted(own, -2)
    sibling = swapped(own)
    other = swapped(early)
    return [early, sibling, own, other, late]


def shards(recordings, pair_blocks, pair_count):
    samples = recordings.reshape(QN, PN, 128)
    own = spectra(pair_blocks[0].T, pair_count, samples)
    rows = pair_rows(gathered(own))
    shared = lax.all_to_all(rows, "tm", 0, 0)
    row = (jnp.sum(shared.astype(F32), axis=0) * (1.0 / math.sqrt(NF * shared.shape[0]))).astype(BF)
    return lag_rows(turned(row, -2))[None].transpose(0, 2, 1, 3)


def solution(mesh):
    in_specs = (P("tm", "fibre", None, None), P("fibre", None, None), P("fibre"))
    out_specs = P("fibre", "tm", None, None)
    return jax.shard_map(shards, mesh=mesh, in_specs=in_specs, out_specs=out_specs, check_vma=False)
```

```python
import functools
import math

import jax
import jax.numpy as jnp
import numpy as np
from jax import lax
from jax.experimental import pallas as pl
from jax.experimental.pallas import tpu as pltpu
from jax.sharding import PartitionSpec as P

TS = 6000
F0 = 60
NF = 1152
MAXLAG = 200
LAGS = 401
VS = 2
REACH = 4
MAXP = 4
EPSILON = 1e-06

QN = 75
PN = 80
KN = 38
KPAD = 40
QPAD = 80
WIDE = 2 * PN + 8
SLOT = 32
GROUP = 2 * SLOT
FN = KN * GROUP
BINS = KN * SLOT
CHUNKS = -(-BINS // 128)
TAIL = 48
ROWS = FN + TAIL
TABLE = ROWS - 1
HALF = 96
RANK = 2 * HALF
STEP = 40
STEPS = PN // STEP
UNROLL = 38
FRONT_VMEM = 28 * 2**20
BF = jnp.bfloat16
F32 = jnp.float32


def cos_table():
    index = np.arange(TS)
    folded = np.minimum(index, TS - index)
    sign = np.where(folded > TS // 4, -1.0, 1.0)
    folded = np.where(folded > TS // 4, TS // 2 - folded, folded)
    square = (folded * (2.0 * math.pi / TS)) ** 2
    value = np.ones(TS)
    for order in range(28, 0, -2):
        value = 1.0 - value * square / (order * (order - 1.0))
    return sign * value


COS = cos_table()


def cosine(index):
    return COS[np.mod(index, TS)]


def sine(index):
    return COS[np.mod(index - TS // 4, TS)]


def split(table, parts=2):
    rest = np.asarray(table, np.float64)
    found = []
    for _ in range(parts):
        found.append(rest.astype(np.float32).astype(BF))
        rest = rest - found[-1].astype(np.float64)
    return found


def bin_slots():
    bins = np.full((KN, SLOT), -1, np.int64)
    flipped = np.zeros((KN, SLOT), bool)
    for residue in range(KN):
        found = [(k, False) for k in range(F0, F0 + NF) if k % QN == residue]
        if residue:
            found += [(k, True) for k in range(F0, F0 + NF) if k % QN == QN - residue]
        for slot, (k, conj) in enumerate(found):
            bins[residue, slot] = k
            flipped[residue, slot] = conj
    return bins, flipped


def first_matrix():
    residue = np.arange(KN)[:, None]
    q = np.arange(QN)[None, :]
    weights = np.zeros((2 * KPAD, QPAD))
    weights[:KN, :QN] = cosine(PN * residue * q)
    weights[KPAD : KPAD + KN, :QN] = -sine(PN * residue * q)
    high, mid, low = split(weights, 3)
    zero = np.zeros_like(low)
    rows = ([high, high, high], [mid, mid, zero], [low, zero, zero])
    return np.concatenate([np.concatenate(row, 1) for row in rows], 0)


def second_matrix():
    bins, flipped = bin_slots()
    p = np.arange(PN)
    weights = np.zeros((KN, GROUP, 2 * PN))
    cos = cosine(bins[:, :, None] * p)
    sin = sine(bins[:, :, None] * p)
    sign = np.where(flipped, -1.0, 1.0)[:, :, None]
    live = (bins >= 0).astype(np.float64)[:, :, None]
    weights[:, :SLOT, :PN] = live * cos
    weights[:, :SLOT, PN:] = live * sign * sin
    weights[:, SLOT:, :PN] = -live * sin
    weights[:, SLOT:, PN:] = live * sign * cos
    return np.concatenate(split(weights, 3), 1)


def basis(table):
    rest = table.copy()
    columns = []
    for _ in range(HALF):
        norms = (rest * rest).sum(0)
        column = rest[:, int(norms.argmax())]
        for _ in range(2):
            for other in columns:
                column = column - other * np.cumsum(other * column)[-1]
        column = column / np.sqrt(np.cumsum(column * column)[-1])
        columns.append(column)
        rest = rest - column[:, None] * (column[:, None] * rest).sum(0)[None]
    return columns


@functools.lru_cache(None)
def lag_factors():
    bins, _ = bin_slots()
    live = (bins >= 0).astype(np.float64)
    lag = np.arange(MAXLAG + 1)[:, None]
    band = np.arange(F0, F0 + NF)[None, :]
    even_table = cosine(lag * band)
    odd_table = sine(lag[1:] * band)
    even = basis(even_table)
    odd = basis(odd_table)
    inner = np.zeros((2, HALF, KN, SLOT))
    place = np.maximum(bins - F0, 0)
    for i in range(HALF):
        inner[0, i] = (even[i][:, None] * even_table).sum(0)[place] * live
        inner[1, i] = (odd[i][:, None] * odd_table).sum(0)[place] * live
    outer = np.zeros((LAGS, RANK))
    for i in range(HALF):
        outer[MAXLAG:, i] = even[i]
        outer[MAXLAG::-1, i] = even[i]
        outer[MAXLAG + 1 :, HALF + i] = -odd[i]
        outer[MAXLAG - 1 :: -1, HALF + i] = odd[i]
    return outer, inner.reshape(RANK, BINS).astype(np.float32)


def thirds(value):
    high = value.astype(BF)
    rest = value - high.astype(F32)
    mid = rest.astype(BF)
    low = (rest - mid.astype(F32)).astype(BF)
    return high, mid, low


def dot(left, right):
    return jnp.dot(left, right, preferred_element_type=F32)


def spectrum_kernel(
    pairs_hbm, count_ref, x_hbm, first_hbm, second_hbm, out_ref,
    pairs_ref, xs, first, second, pad, ts, zs, ss, sems,
):
    def load(g):
        return pltpu.make_async_copy(
            x_hbm.at[:, pl.ds(g * STEP, STEP), :], xs.at[g, pl.ds(0, QN)], sems.at[g]
        )

    first_copy = pltpu.make_async_copy(first_hbm, first, sems.at[STEPS])
    second_copy = pltpu.make_async_copy(second_hbm, second, sems.at[STEPS + 1])
    first_copy.start()
    for g in range(STEPS):
        load(g).start()
    second_copy.start()
    pairs_copy = pltpu.make_async_copy(pairs_hbm, pairs_ref, sems.at[STEPS + 2])
    pairs_copy.start()
    pad[72:80, :] = jnp.zeros((8, STEP * 128), F32)

    def sections(g, carry):
        load(g).wait()
        flat = xs.at[g].reshape((QN + 1) * STEP, 128)
        for s in range(STEP):
            pad[0:QN, s * 128 : (s + 1) * 128] = flat[pl.ds(s, QN, stride=STEP), :]
        for pair in range(STEP // 2):
            parts = thirds(pad[:, pair * 256 : (pair + 1) * 256])
            full = dot(first[...], jnp.concatenate(parts, 0))
            section = full[: 2 * KPAD] + (full[2 * KPAD : 4 * KPAD] + full[4 * KPAD :])
            for side in range(2):
                p = g * STEP + pair * 2 + side
                part = section[:, side * 128 : (side + 1) * 128]
                ts[pl.ds(p, KPAD, stride=WIDE), :] = part[:KPAD]
                ts[pl.ds(PN + p, KPAD, stride=WIDE), :] = part[KPAD:]
        return carry

    first_copy.wait()
    lax.fori_loop(0, STEPS, sections, 0)
    second_copy.wait()

    def residue(k, power):
        high, mid, low = thirds(ts[pl.ds(pl.multiple_of(k * WIDE, 8), 2 * PN), :])
        table = second[k]
        wide = dot(table, jnp.concatenate([high, mid], 1))
        small = wide[:GROUP, 128:] + wide[GROUP : 2 * GROUP, :128]
        least = wide[GROUP : 2 * GROUP, 128:] + wide[2 * GROUP :, :128] + dot(table[:GROUP], low)
        value = wide[:GROUP, :128] + (small + least)
        at = pl.multiple_of(k * SLOT, SLOT)
        zs[pl.ds(at, SLOT), :] = value[:SLOT]
        zs[pl.ds(BINS + at, SLOT), :] = value[SLOT:]
        return power + jnp.sum((value * value).reshape(GROUP // 8, 8, 128), axis=0)

    power = lax.fori_loop(0, KN, residue, jnp.zeros((8, 128), F32), unroll=UNROLL)
    power = jnp.sum(power, axis=0, keepdims=True)
    factor = lax.rsqrt(power * (1.0 / NF) + EPSILON)
    out_ref[0:FN, :] = (zs[...] * factor).astype(BF)
    lane = lax.broadcasted_iota(jnp.int32, (8, 128), 1)
    sub = lax.broadcasted_iota(jnp.int32, (8, 128), 0)
    pick = jnp.where(lane == sub * (128 // VS), 1.0, 0.0).astype(BF)
    ss[...] = jnp.zeros_like(ss)
    for part in range(2):
        rows = lax.dot_general(
            pick,
            out_ref[part * BINS : (part + 1) * BINS, :],
            (((1,), (1,)), ((), ())),
            preferred_element_type=F32,
        )
        for j in range(VS):
            for c in range(CHUNKS):
                at = (j * 2 + part) * CHUNKS + c
                wide = min(128, BINS - c * 128)
                ss[at : at + 1, 0:wide] = rows[j : j + 1, c * 128 : c * 128 + wide]
    pairs_copy.wait()
    owner = lax.axis_index("fibre")
    lane = lax.broadcasted_iota(jnp.int32, (1, 128), 1)
    table = jnp.where(lane == 2 * MAXP, count_ref[0], 0)
    for slot in range(MAXP):
        for side in range(2):
            offset = pairs_ref[side, slot] - owner
            table = jnp.where(lane == slot * 2 + side, offset, table)
    ss[TABLE - FN : TABLE - FN + 1, :] = table.astype(F32)
    out_ref[FN:ROWS, :] = ss[...].astype(BF)


def in_hbm(array):
    return pltpu.with_memory_space_constraint(array, pltpu.HBM)


def spectra(pair_blocks, pair_count, samples):
    vmem = pl.BlockSpec(memory_space=pltpu.VMEM)
    hbm = pl.BlockSpec(memory_space=pltpu.HBM)
    first = jnp.asarray(first_matrix())
    second = jnp.asarray(second_matrix())
    return pl.pallas_call(
        spectrum_kernel,
        in_specs=[hbm, pl.BlockSpec(memory_space=pltpu.SMEM), hbm, hbm, hbm],
        out_specs=vmem,
        out_shape=jax.ShapeDtypeStruct((ROWS, 128), BF),
        scratch_shapes=[
            pltpu.SMEM(pair_blocks.shape, jnp.int32),
            pltpu.VMEM((STEPS, QN + 1, STEP, 128), F32),
            pltpu.VMEM(first.shape, BF),
            pltpu.VMEM(second.shape, BF),
            pltpu.VMEM((QPAD, STEP * 128), F32),
            pltpu.VMEM(((KPAD + 1) * WIDE, 128), F32),
            pltpu.VMEM((FN, 128), F32),
            pltpu.VMEM((TAIL, 128), F32),
            pltpu.SemaphoreType.DMA((STEPS + 3,)),
        ],
        compiler_params=pltpu.CompilerParams(vmem_limit_bytes=FRONT_VMEM),
        name="spectra",
    )(
        in_hbm(pair_blocks), pair_count, in_hbm(samples), in_hbm(first), in_hbm(second)
    )


def pairs_kernel(
    b0, b1, b2, b3, b4, inner_ref, out_ref, entries, receiver, source, weights
):
    blocks = (b0, b1, b2, b3, b4)
    even = lax.rem(lax.axis_index("fibre"), 2) == 0
    tail = jnp.where(even, b4[FN:ROWS, :].astype(F32), b0[FN:ROWS, :].astype(F32))
    row = tail[TABLE - FN : TABLE - FN + 1, :].astype(jnp.int32)
    lane = lax.broadcasted_iota(jnp.int32, (1, 128), 1)
    for index in range(2 * MAXP + 1):
        entries[index] = jnp.sum(jnp.where(lane == index, row, 0))

    def place_of(offset):
        return jnp.where(even, REACH - offset, offset)

    count = entries[2 * MAXP]

    def one_pair(slot, carry):
        first = place_of(entries[2 * slot])
        second = place_of(entries[2 * slot + 1])
        for place, block in enumerate(blocks):

            @pl.when(second == place)
            def _():
                receiver[:, 0:128] = block[0:BINS, :]
                receiver[:, 128:256] = block[BINS:FN, :]

            @pl.when(first == place)
            def _():
                source[...] = block[FN:ROWS, :].astype(F32)

        for c in range(CHUNKS):
            wide = min(128, BINS - c * 128)
            here = slice(c * 128, c * 128 + wide)
            table = inner_ref[:, here]
            for part in range(2 * VS):
                at = part * CHUNKS + c
                scaled = table * source[at : at + 1, 0:wide]
                weights[part * RANK : (part + 1) * RANK, here] = scaled.astype(BF)
        product = dot(weights[...], receiver[...])
        for j in range(VS):
            real = product[(2 * j) * RANK : (2 * j + 1) * RANK]
            imag = product[(2 * j + 1) * RANK : (2 * j + 2) * RANK]
            same = real[:HALF, :128] + imag[:HALF, 128:]
            turn = real[HALF:, 128:] - imag[HALF:, :128]
            out_ref[slot * VS + j, 0:HALF, :] = same.astype(BF)
            out_ref[slot * VS + j, HALF:RANK, :] = turn.astype(BF)
        return carry

    def one_blank(slot, carry):
        for j in range(VS):
            out_ref[slot * VS + j] = jnp.zeros((RANK, 128), BF)
        return carry

    lax.fori_loop(0, count, one_pair, 0)
    lax.fori_loop(count, MAXP, one_blank, 0)


def pair_rows(blocks):
    _, inner = lag_factors()
    vmem = pl.BlockSpec(memory_space=pltpu.VMEM)
    return pl.pallas_call(
        pairs_kernel,
        in_specs=[vmem] * 6,
        out_specs=vmem,
        out_shape=jax.ShapeDtypeStruct((MAXP * VS, RANK, 128), BF),
        scratch_shapes=[
            pltpu.SMEM((2 * MAXP + 1,), jnp.int32),
            pltpu.VMEM((BINS, 256), BF),
            pltpu.VMEM((TAIL, 128), F32),
            pltpu.VMEM((2 * VS * RANK, BINS), BF),
        ],
        compiler_params=pltpu.CompilerParams(vmem_limit_bytes=28 * 2**20),
        name="pair_rows",
    )(*blocks, jnp.asarray(inner))


def lags_kernel(row_ref, outer_ref, out_ref):
    row = row_ref[...]
    out_ref[:, 0, :] = dot(outer_ref[...], jnp.concatenate([row, row], 0))


def lag_rows(row):
    outer, _ = lag_factors()
    high, low = split(outer)
    table = jnp.asarray(np.concatenate([high, low], 1))
    vmem = pl.BlockSpec(memory_space=pltpu.VMEM)
    return pl.pallas_call(
        lags_kernel,
        in_specs=[vmem, vmem],
        out_specs=vmem,
        out_shape=jax.ShapeDtypeStruct((LAGS, 1, 128), F32),
        compiler_params=pltpu.CompilerParams(vmem_limit_bytes=8 * 2**20),
        name="lag_rows",
    )(row, table)


def turned(array, by):
    size = lax.axis_size("fibre")
    return lax.ppermute(array, "fibre", [(i, (i + by) % size) for i in range(size)])


def swapped(array):
    size = lax.axis_size("fibre")
    return lax.ppermute(array, "fibre", [(i, i ^ 1) for i in range(size)])


def parted(array, by):
    size = lax.axis_size("fibre")
    return lax.ppermute(
        array, "fibre", [(i, (i - by if i % 2 == 0 else i + by) % size) for i in range(size)]
    )


def gathered(own):
    early = parted(own, 2)
    late = parted(own, -2)
    sibling = swapped(own)
    other = swapped(early)
    return [early, sibling, own, other, late]


def shards(recordings, pair_blocks, pair_count):
    samples = recordings.reshape(QN, PN, 128)
    own = spectra(pair_blocks[0].T, pair_count, samples)
    rows = pair_rows(gathered(own))
    shared = lax.all_to_all(rows, "tm", 0, 0)
    row = (jnp.sum(shared.astype(F32), axis=0) * (1.0 / math.sqrt(NF * shared.shape[0]))).astype(BF)
    return lag_rows(turned(row, -2))[None].transpose(0, 2, 1, 3)


def solution(mesh):
    in_specs = (P("tm", "fibre", None, None), P("fibre", None, None), P("fibre"))
    out_specs = P("fibre", "tm", None, None)
    return jax.shard_map(shards, mesh=mesh, in_specs=in_specs, out_specs=out_specs, check_vma=False)
```

```python
import functools
import math

import jax
import jax.numpy as jnp
import numpy as np
from jax import lax
from jax.experimental import pallas as pl
from jax.experimental.pallas import tpu as pltpu
from jax.sharding import PartitionSpec as P

TS = 6000
F0 = 60
NF = 1152
MAXLAG = 200
LAGS = 401
VS = 2
REACH = 4
MAXP = 4
EPSILON = 1e-06

QN = 75
PN = 80
KN = 38
KPAD = 40
QPAD = 80
WIDE = 2 * PN + 8
SLOT = 32
GROUP = 2 * SLOT
FN = KN * GROUP
BINS = KN * SLOT
CHUNKS = -(-BINS // 128)
TAIL = 48
ROWS = FN + TAIL
TABLE = ROWS - 1
HALF = 96
RANK = 2 * HALF
STEP = 40
STEPS = PN // STEP
UNROLL = 38
FRONT_VMEM = 28 * 2**20
BF = jnp.bfloat16
F32 = jnp.float32


def cos_table():
    index = np.arange(TS)
    folded = np.minimum(index, TS - index)
    sign = np.where(folded > TS // 4, -1.0, 1.0)
    folded = np.where(folded > TS // 4, TS // 2 - folded, folded)
    square = (folded * (2.0 * math.pi / TS)) ** 2
    value = np.ones(TS)
    for order in range(28, 0, -2):
        value = 1.0 - value * square / (order * (order - 1.0))
    return sign * value


COS = cos_table()


def cosine(index):
    return COS[np.mod(index, TS)]


def sine(index):
    return COS[np.mod(index - TS // 4, TS)]


def split(table, parts=2):
    rest = np.asarray(table, np.float64)
    found = []
    for _ in range(parts):
        found.append(rest.astype(np.float32).astype(BF))
        rest = rest - found[-1].astype(np.float64)
    return found


def bin_slots():
    bins = np.full((KN, SLOT), -1, np.int64)
    flipped = np.zeros((KN, SLOT), bool)
    for residue in range(KN):
        found = [(k, False) for k in range(F0, F0 + NF) if k % QN == residue]
        if residue:
            found += [(k, True) for k in range(F0, F0 + NF) if k % QN == QN - residue]
        for slot, (k, conj) in enumerate(found):
            bins[residue, slot] = k
            flipped[residue, slot] = conj
    return bins, flipped


def first_matrix():
    residue = np.arange(KN)[:, None]
    q = np.arange(QN)[None, :]
    weights = np.zeros((2 * KPAD, QPAD))
    weights[:KN, :QN] = cosine(PN * residue * q)
    weights[KPAD : KPAD + KN, :QN] = -sine(PN * residue * q)
    high, mid, low = split(weights, 3)
    zero = np.zeros_like(low)
    rows = ([high, high, high], [mid, mid, zero], [low, zero, zero])
    return np.concatenate([np.concatenate(row, 1) for row in rows], 0)


def second_matrix():
    bins, flipped = bin_slots()
    p = np.arange(PN)
    weights = np.zeros((KN, GROUP, 2 * PN))
    cos = cosine(bins[:, :, None] * p)
    sin = sine(bins[:, :, None] * p)
    sign = np.where(flipped, -1.0, 1.0)[:, :, None]
    live = (bins >= 0).astype(np.float64)[:, :, None]
    weights[:, :SLOT, :PN] = live * cos
    weights[:, :SLOT, PN:] = live * sign * sin
    weights[:, SLOT:, :PN] = -live * sin
    weights[:, SLOT:, PN:] = live * sign * cos
    return np.concatenate(split(weights, 3), 1)


def basis(table):
    rest = table.copy()
    columns = []
    for _ in range(HALF):
        norms = (rest * rest).sum(0)
        column = rest[:, int(norms.argmax())]
        for _ in range(2):
            for other in columns:
                column = column - other * np.cumsum(other * column)[-1]
        column = column / np.sqrt(np.cumsum(column * column)[-1])
        columns.append(column)
        rest = rest - column[:, None] * (column[:, None] * rest).sum(0)[None]
    return columns


@functools.lru_cache(None)
def lag_factors():
    bins, _ = bin_slots()
    live = (bins >= 0).astype(np.float64)
    lag = np.arange(MAXLAG + 1)[:, None]
    band = np.arange(F0, F0 + NF)[None, :]
    even_table = cosine(lag * band)
    odd_table = sine(lag[1:] * band)
    even = basis(even_table)
    odd = basis(odd_table)
    inner = np.zeros((2, HALF, KN, SLOT))
    place = np.maximum(bins - F0, 0)
    for i in range(HALF):
        inner[0, i] = (even[i][:, None] * even_table).sum(0)[place] * live
        inner[1, i] = (odd[i][:, None] * odd_table).sum(0)[place] * live
    outer = np.zeros((LAGS, RANK))
    for i in range(HALF):
        outer[MAXLAG:, i] = even[i]
        outer[MAXLAG::-1, i] = even[i]
        outer[MAXLAG + 1 :, HALF + i] = -odd[i]
        outer[MAXLAG - 1 :: -1, HALF + i] = odd[i]
    return outer, inner.reshape(RANK, BINS).astype(np.float32)


def thirds(value):
    high = value.astype(BF)
    rest = value - high.astype(F32)
    mid = rest.astype(BF)
    low = (rest - mid.astype(F32)).astype(BF)
    return high, mid, low


def dot(left, right):
    return jnp.dot(left, right, preferred_element_type=F32)


def spectrum_kernel(
    pairs_hbm, count_ref, x_hbm, first_hbm, second_hbm, out_ref,
    pairs_ref, xs, first, second, pad, ts, zs, ss, sems,
):
    def load(g):
        return pltpu.make_async_copy(
            x_hbm.at[:, pl.ds(g * STEP, STEP), :], xs.at[g, pl.ds(0, QN)], sems.at[g]
        )

    first_copy = pltpu.make_async_copy(first_hbm, first, sems.at[STEPS])
    second_copy = pltpu.make_async_copy(second_hbm, second, sems.at[STEPS + 1])
    first_copy.start()
    for g in range(STEPS):
        load(g).start()
    second_copy.start()
    pairs_copy = pltpu.make_async_copy(pairs_hbm, pairs_ref, sems.at[STEPS + 2])
    pairs_copy.start()
    pad[72:80, :] = jnp.zeros((8, STEP * 128), F32)

    def sections(g, carry):
        load(g).wait()
        flat = xs.at[g].reshape((QN + 1) * STEP, 128)
        for s in range(STEP):
            pad[0:QN, s * 128 : (s + 1) * 128] = flat[pl.ds(s, QN, stride=STEP), :]
        for pair in range(STEP // 2):
            parts = thirds(pad[:, pair * 256 : (pair + 1) * 256])
            full = dot(first[...], jnp.concatenate(parts, 0))
            section = full[: 2 * KPAD] + (full[2 * KPAD : 4 * KPAD] + full[4 * KPAD :])
            for side in range(2):
                p = g * STEP + pair * 2 + side
                part = section[:, side * 128 : (side + 1) * 128]
                ts[pl.ds(p, KPAD, stride=WIDE), :] = part[:KPAD]
                ts[pl.ds(PN + p, KPAD, stride=WIDE), :] = part[KPAD:]
        return carry

    first_copy.wait()
    lax.fori_loop(0, STEPS, sections, 0)
    second_copy.wait()

    def residue(k, power):
        high, mid, low = thirds(ts[pl.ds(pl.multiple_of(k * WIDE, 8), 2 * PN), :])
        table = second[k]
        wide = dot(table, jnp.concatenate([high, mid], 1))
        small = wide[:GROUP, 128:] + wide[GROUP : 2 * GROUP, :128]
        least = wide[GROUP : 2 * GROUP, 128:] + wide[2 * GROUP :, :128] + dot(table[:GROUP], low)
        value = wide[:GROUP, :128] + (small + least)
        at = pl.multiple_of(k * SLOT, SLOT)
        zs[pl.ds(at, SLOT), :] = value[:SLOT]
        zs[pl.ds(BINS + at, SLOT), :] = value[SLOT:]
        return power + jnp.sum((value * value).reshape(GROUP // 8, 8, 128), axis=0)

    power = lax.fori_loop(0, KN, residue, jnp.zeros((8, 128), F32), unroll=UNROLL)
    power = jnp.sum(power, axis=0, keepdims=True)
    factor = lax.rsqrt(power * (1.0 / NF) + EPSILON)
    out_ref[0:FN, :] = (zs[...] * factor).astype(BF)
    lane = lax.broadcasted_iota(jnp.int32, (8, 128), 1)
    sub = lax.broadcasted_iota(jnp.int32, (8, 128), 0)
    pick = jnp.where(lane == sub * (128 // VS), 1.0, 0.0).astype(BF)
    ss[...] = jnp.zeros_like(ss)
    for part in range(2):
        rows = lax.dot_general(
            pick,
            out_ref[part * BINS : (part + 1) * BINS, :],
            (((1,), (1,)), ((), ())),
            preferred_element_type=F32,
        )
        for j in range(VS):
            for c in range(CHUNKS):
                at = (j * 2 + part) * CHUNKS + c
                wide = min(128, BINS - c * 128)
                ss[at : at + 1, 0:wide] = rows[j : j + 1, c * 128 : c * 128 + wide]
    pairs_copy.wait()
    owner = lax.axis_index("fibre")
    lane = lax.broadcasted_iota(jnp.int32, (1, 128), 1)
    table = jnp.where(lane == 2 * MAXP, count_ref[0], 0)
    for slot in range(MAXP):
        for side in range(2):
            offset = pairs_ref[side, slot] - owner
            table = jnp.where(lane == slot * 2 + side, offset, table)
    ss[TABLE - FN : TABLE - FN + 1, :] = table.astype(F32)
    out_ref[FN:ROWS, :] = ss[...].astype(BF)


def in_hbm(array):
    return pltpu.with_memory_space_constraint(array, pltpu.HBM)


def spectra(pair_blocks, pair_count, samples):
    vmem = pl.BlockSpec(memory_space=pltpu.VMEM)
    hbm = pl.BlockSpec(memory_space=pltpu.HBM)
    first = jnp.asarray(first_matrix())
    second = jnp.asarray(second_matrix())
    return pl.pallas_call(
        spectrum_kernel,
        in_specs=[hbm, pl.BlockSpec(memory_space=pltpu.SMEM), hbm, hbm, hbm],
        out_specs=vmem,
        out_shape=jax.ShapeDtypeStruct((ROWS, 128), BF),
        scratch_shapes=[
            pltpu.SMEM(pair_blocks.shape, jnp.int32),
            pltpu.VMEM((STEPS, QN + 1, STEP, 128), F32),
            pltpu.VMEM(first.shape, BF),
            pltpu.VMEM(second.shape, BF),
            pltpu.VMEM((QPAD, STEP * 128), F32),
            pltpu.VMEM(((KPAD + 1) * WIDE, 128), F32),
            pltpu.VMEM((FN, 128), F32),
            pltpu.VMEM((TAIL, 128), F32),
            pltpu.SemaphoreType.DMA((STEPS + 3,)),
        ],
        compiler_params=pltpu.CompilerParams(vmem_limit_bytes=FRONT_VMEM),
        name="spectra",
    )(
        in_hbm(pair_blocks), pair_count, in_hbm(samples), in_hbm(first), in_hbm(second)
    )


def pairs_kernel(
    b0, b1, b2, b3, b4, inner_ref, out_ref, entries, receiver, source, weights
):
    blocks = (b0, b1, b2, b3, b4)
    even = lax.rem(lax.axis_index("fibre"), 2) == 0
    tail = jnp.where(even, b4[FN:ROWS, :].astype(F32), b0[FN:ROWS, :].astype(F32))
    row = tail[TABLE - FN : TABLE - FN + 1, :].astype(jnp.int32)
    lane = lax.broadcasted_iota(jnp.int32, (1, 128), 1)
    for index in range(2 * MAXP + 1):
        entries[index] = jnp.sum(jnp.where(lane == index, row, 0))

    def place_of(offset):
        return jnp.where(even, REACH - offset, offset)

    count = entries[2 * MAXP]

    def one_pair(slot, carry):
        first = place_of(entries[2 * slot])
        second = place_of(entries[2 * slot + 1])
        for place, block in enumerate(blocks):

            @pl.when(second == place)
            def _():
                receiver[:, 0:128] = block[0:BINS, :]
                receiver[:, 128:256] = block[BINS:FN, :]

            @pl.when(first == place)
            def _():
                source[...] = block[FN:ROWS, :].astype(F32)

        for c in range(CHUNKS):
            wide = min(128, BINS - c * 128)
            here = slice(c * 128, c * 128 + wide)
            table = inner_ref[:, here]
            for part in range(2 * VS):
                at = part * CHUNKS + c
                scaled = table * source[at : at + 1, 0:wide]
                weights[part * RANK : (part + 1) * RANK, here] = scaled.astype(BF)
        product = dot(weights[...], receiver[...])
        for j in range(VS):
            real = product[(2 * j) * RANK : (2 * j + 1) * RANK]
            imag = product[(2 * j + 1) * RANK : (2 * j + 2) * RANK]
            same = real[:HALF, :128] + imag[:HALF, 128:]
            turn = real[HALF:, 128:] - imag[HALF:, :128]
            out_ref[slot * VS + j, 0:HALF, :] = same.astype(BF)
            out_ref[slot * VS + j, HALF:RANK, :] = turn.astype(BF)
        return carry

    def one_blank(slot, carry):
        for j in range(VS):
            out_ref[slot * VS + j] = jnp.zeros((RANK, 128), BF)
        return carry

    lax.fori_loop(0, count, one_pair, 0)
    lax.fori_loop(count, MAXP, one_blank, 0)


def pair_rows(blocks):
    _, inner = lag_factors()
    vmem = pl.BlockSpec(memory_space=pltpu.VMEM)
    return pl.pallas_call(
        pairs_kernel,
        in_specs=[vmem] * 6,
        out_specs=vmem,
        out_shape=jax.ShapeDtypeStruct((MAXP * VS, RANK, 128), BF),
        scratch_shapes=[
            pltpu.SMEM((2 * MAXP + 1,), jnp.int32),
            pltpu.VMEM((BINS, 256), BF),
            pltpu.VMEM((TAIL, 128), F32),
            pltpu.VMEM((2 * VS * RANK, BINS), BF),
        ],
        compiler_params=pltpu.CompilerParams(vmem_limit_bytes=28 * 2**20),
        name="pair_rows",
    )(*blocks, jnp.asarray(inner))


def lags_kernel(row_ref, outer_ref, out_ref):
    row = row_ref[...]
    out_ref[:, 0, :] = dot(outer_ref[...], jnp.concatenate([row, row], 0))


def lag_rows(row):
    outer, _ = lag_factors()
    high, low = split(outer)
    table = jnp.asarray(np.concatenate([high, low], 1))
    vmem = pl.BlockSpec(memory_space=pltpu.VMEM)
    return pl.pallas_call(
        lags_kernel,
        in_specs=[vmem, vmem],
        out_specs=vmem,
        out_shape=jax.ShapeDtypeStruct((LAGS, 1, 128), F32),
        compiler_params=pltpu.CompilerParams(vmem_limit_bytes=8 * 2**20),
        name="lag_rows",
    )(row, table)


def turned(array, by):
    size = lax.axis_size("fibre")
    return lax.ppermute(array, "fibre", [(i, (i + by) % size) for i in range(size)])


def swapped(array):
    size = lax.axis_size("fibre")
    return lax.ppermute(array, "fibre", [(i, i ^ 1) for i in range(size)])


def parted(array, by):
    size = lax.axis_size("fibre")
    steps = [(i, i - by if i % 2 == 0 else i + by) for i in range(size)]
    return lax.ppermute(array, "fibre", [(i, to % size) for i, to in steps if to >= 0])


def gathered(own):
    early = parted(own, 2)
    late = parted(own, -2)
    sibling = swapped(own)
    other = swapped(early)
    return [early, sibling, own, other, late]


def shards(recordings, pair_blocks, pair_count):
    samples = recordings.reshape(QN, PN, 128)
    own = spectra(pair_blocks[0].T, pair_count, samples)
    rows = pair_rows(gathered(own))
    shared = lax.all_to_all(rows, "tm", 0, 0)
    row = (jnp.sum(shared.astype(F32), axis=0) * (1.0 / math.sqrt(NF * shared.shape[0]))).astype(BF)
    return lag_rows(turned(row, -2))[None].transpose(0, 2, 1, 3)


def solution(mesh):
    in_specs = (P("tm", "fibre", None, None), P("fibre", None, None), P("fibre"))
    out_specs = P("fibre", "tm", None, None)
    return jax.shard_map(shards, mesh=mesh, in_specs=in_specs, out_specs=out_specs, check_vma=False)
```
